32 devices in a mesh: gx: 4 (over y, x), vert: 8 (over z, core).
Axes of the slice: x: 2, y: 2, z: 4, core: 2. Of those that a mesh axis runs over, the one named last changes fastest.
Arguments:
- dist: float32 [2, 4096, 24576], P(None, 'vert', 'gx'), may hold values from -6 to 6
- factors: float32 [2, 4096, 128], P(None, 'vert', 'gx'), may hold values from 0.95 to 0.999
- velocity: float32 [3, 2, 4096], P(None, None, 'vert'), may hold values from -3 to 3
- weights: float32 [13, 2, 4096], P(None, None, 'vert'), may hold values from -0.0625 to 0.0625
- relax: float32 [2, 4096], P(None, 'vert'), may hold values from 0.1 to 0.9
Outputs:
- updated: float32 [2, 4096, 24576], P(None, 'vert', 'gx')
- macro: float32 [13, 24576], P(None, 'gx')
The draws below stay inside these ranges and needn't reach their ends.
All inputs are finite; a program needn't handle non-finite values.
Results may differ from the reference program's by a relative error of at most 0.000071.
Values sent between devices are 32-bit elements; how exact they have to be, the bound alone decides.
No kernel may reach another device: no remote copies, remote signals or barrier semaphores. Data moves between devices by JAX's collectives and lax.ppermute only.
A program may use at most 192 MiB of HBM per device.

```python
import math
import jax
import jax.numpy as jnp
from jax import lax

VEL = 4096
K = 13
SMOOTH = 4
YZ = 192
NX = 128
CELLS = 24576


def shard_levels(stream_key, dims, split, least, largest):
    level = 1.0
    for dim, blocks in split:
        steps = jax.random.uniform(jax.random.fold_in(jax.random.fold_in(stream_key, 6), dim), (blocks,), jnp.float32, least / len(split), largest / len(split))
        level = level * jnp.repeat(jnp.exp(steps), dims[dim] // blocks).reshape((-1,) + (1,) * (len(dims) - 1 - dim))
    return level


def scatter_about(key, extent, spread, reach, cuts=(), dtype=jnp.bfloat16):
    array = jax.random.normal(key, extent, jnp.float32) * spread
    if len(cuts) > 0:
        array = shard_levels(key, extent, cuts, -0.22, 0.18) * array
    return jnp.clip(array, min=-reach, max=reach).astype(dtype)


def setup_inputs(seed: int = 0) -> dict:
    arg_keys = jax.random.split(jax.random.key(seed), 6)
    return {
        "dist": scatter_about(arg_keys[0], (2, VEL, CELLS), 1.0, 6.0, ((1, 8), (2, 4)), jnp.float32),
        "factors": jnp.clip(jnp.exp(math.log(0.999) - 0.05029282 * jax.random.uniform(arg_keys[1], (2, VEL, NX), jnp.float32) ** shard_levels(arg_keys[1], (2, VEL, NX), ((1, 8), (2, 4)), -0.2, 0.2)), 0.95, 0.999),
        "velocity": jnp.clip(jax.random.uniform(arg_keys[2], (3, 2, VEL), jnp.float32, -3.0, 3.0) * shard_levels(arg_keys[2], (3, 2, VEL), ((2, 8),), -0.4, 0.0), -3.0, 3.0),
        "weights": scatter_about(arg_keys[3], (K, 2, VEL), (2 * VEL) ** -0.5, 0.0625, ((2, 8),), jnp.float32),
        "relax": jnp.clip(jnp.exp(math.log(0.9) - 2.1972245 * jax.random.uniform(arg_keys[4], (2, VEL), jnp.float32) ** shard_levels(arg_keys[4], (2, VEL), ((1, 8),), -0.2, 0.2)), 0.1, 0.9),
    }


smooth_rate = 0.24

def equilibrium(moments, speed_x, speed_y, speed_z):
    density = 1.0 + 0.5 * jnp.tanh(moments[0])
    flow_x = 0.5 * jnp.tanh(moments[1])
    flow_y = 0.5 * jnp.tanh(moments[2])
    flow_z = 0.5 * jnp.tanh(moments[3])
    temper = 1.0 + 0.5 * jnp.tanh(moments[4])
    stress = 0.2 * jnp.tanh(moments[5:10])
    fluxes = 0.2 * jnp.tanh(moments[10:13])
    rel_x = speed_x - flow_x
    rel_y = speed_y - flow_y
    rel_z = speed_z - flow_z
    square = rel_x * rel_x + rel_y * rel_y + rel_z * rel_z
    inverse = 1.0 / temper
    shape_term = stress[0] * rel_x * rel_y + stress[1] * rel_x * rel_z + stress[2] * rel_y * rel_z + 0.5 * stress[3] * (rel_x * rel_x - rel_z * rel_z) + 0.5 * stress[4] * (rel_y * rel_y - rel_z * rel_z)
    heat_term = (fluxes[0] * rel_x + fluxes[1] * rel_y + fluxes[2] * rel_z) * (0.5 * square * inverse - 2.5)
    return density * inverse * jnp.sqrt(inverse) * jnp.exp(-0.5 * square * inverse) * (1.0 + (shape_term + heat_term) * inverse)

def sweep_direction(rates, source, reverse):

    def advance(carry, item):
        rate, term = item
        value = rate[:, None] * carry + term
        return (value, value)
    start = jnp.zeros((source.shape[0], source.shape[2]), jnp.float32)
    _, values = lax.scan(advance, start, (rates.T, jnp.moveaxis(source, 1, 0)), reverse=reverse)
    return jnp.moveaxis(values, 0, 1)

def reference(dist, factors, velocity, weights, relax):
    grid = dist.reshape(2, VEL, NX, YZ)
    source = jnp.sqrt(1.0 - factors * factors)[..., None] * grid
    swept = jnp.stack([sweep_direction(factors[0], source[0], False), sweep_direction(factors[1], source[1], True)])
    moments = jnp.einsum('kdv,dvxc->kxc', weights, swept, precision=lax.Precision.HIGHEST)
    for step in range(SMOOTH):
        padded = jnp.pad(moments, ((0, 0), (1, 1), (0, 0)))
        coef = 1.0 / (1.0 + moments[0] * moments[0])
        moments = moments + smooth_rate * coef * (padded[:, 2:] - 2.0 * moments + padded[:, :-2])

    def relax_one(item):
        values, speeds, fraction = item
        equil = equilibrium(moments, speeds[0][:, None, None], speeds[1][:, None, None], speeds[2][:, None, None])
        return values + fraction[:, None, None] * (equil - values)
    result = lax.map(relax_one, (jnp.moveaxis(swept, 1, 0), jnp.moveaxis(velocity, 2, 0), relax.T))
    updated = jnp.moveaxis(result, 0, 1).reshape(2, VEL, NX * YZ)
    return (updated, moments.reshape(K, NX * YZ))
```

```python
import jax
import jax.numpy as jnp
from jax import lax
from jax.experimental import pallas as pl
from jax.experimental.pallas import tpu as pltpu
from jax.sharding import PartitionSpec as P

SMOOTH = 4
RATE = 0.24
LANES = 128
PARTS = 2
SUB = 32
MIB = 2**20

f32 = jnp.float32
bf16 = jnp.bfloat16


def dot(a, b):
    return jnp.dot(a, b, preferred_element_type=f32)


def halves(x):
    high = x.astype(bf16)
    return high, (x - high.astype(f32)).astype(bf16)


def thirds(x):
    high = x.astype(bf16)
    rest = x - high.astype(f32)
    middle = rest.astype(bf16)
    return high, middle, (rest - middle.astype(f32)).astype(bf16)


def rounded(x):
    return lax.reduce_precision(x, 8, 7)


def outside_thirds(x):
    high = rounded(x)
    middle = rounded(x - high)
    return high.astype(bf16), middle.astype(bf16), rounded(x - high - middle).astype(bf16)


def low_half(rows):
    return lax.broadcasted_iota(jnp.int32, (rows, LANES), 1) < LANES // 2


def turn(x):
    return pltpu.roll(x, LANES // 2, 1)


def swap_cells(pair, whole, low):
    tiles = len(pair)
    turned = [turn(t) for t in pair]
    return [
        jnp.where(low, turned[(t + whole) % tiles], turned[(t + whole + 1) % tiles])
        for t in range(tiles)
    ]


def by_cell(first, second, tiles, whole, low):
    mixed = jnp.where(low, first, second)
    return [first if t < whole else mixed if t == whole else second for t in range(tiles)]


def sweep_rows(rows, load, store, gain, reach, backward, pairs, plane):
    tiles, whole = 2 * plane // LANES, plane // LANES
    low = low_half(rows)
    zero = jnp.zeros((rows, LANES), f32)
    sums, late = [zero] * tiles, [zero] * tiles
    for step in range(pairs):
        p = pairs - 1 - step if backward else step
        spread = lambda c: jnp.broadcast_to(c, (rows, LANES))
        g = by_cell(spread(gain[:, 2 * p : 2 * p + 1]), spread(gain[:, 2 * p + 1 : 2 * p + 2]), tiles, whole, low)
        r = by_cell(spread(reach[:, 2 * p : 2 * p + 1]), spread(reach[:, 2 * p + 1 : 2 * p + 2]), tiles, whole, low)
        term = [g[t] * load(p, t) for t in range(tiles)]
        early = []
        total = []
        for t in range(tiles):
            if t == whole:
                now, then = (term[t], late[t]) if not backward else (late[t], term[t])
                early.append(sums[t] + jnp.where(low, now, then))
                total.append(jnp.where(low, 0.0, term[t]) if not backward else jnp.where(low, term[t], 0.0))
            elif (t < whole) != backward:
                early.append(sums[t] + term[t])
                total.append(None)
            else:
                early.append(sums[t] + late[t])
                total.append(term[t])
        sums, late = early, term
        crossed = swap_cells(sums, whole, low)
        values = []
        for t in range(tiles):
            value = sums[t] + crossed[t]
            if total[t] is not None:
                value = value + total[t]
            values.append(r[t] * value)
            store(p, t, values[t])
    return values


def packed_last(values, backward, whole, low):
    tiles = len(values)
    if backward:
        return values[:whole], values[whole]
    turned = [turn(v) for v in values[whole:]]
    full = [jnp.where(low, turned[i], turned[i + 1]) for i in range(whole)]
    return full, turned[whole]


def sweep_kernel(part, block, plane, dist, coef, *rest):
    others = len(rest) - 1
    swept, sent = rest[0], rest[1:]
    count = others + 1
    me = lax.axis_index("gx")
    vel = swept.shape[1]
    cells = swept.shape[2] // plane
    pairs = cells // 2
    tiles, whole = 2 * plane // LANES, plane // LANES
    width = 2 * plane
    offset = part * (vel // block)

    def body(ahead, back):
        step = pl.program_id(0)
        for sub in range(block // SUB):
            here = slice(sub * SUB, (sub + 1) * SUB)
            row = pl.multiple_of(step * block + sub * SUB, SUB)
            leaving = []
            for d, ref in enumerate((ahead, back)):
                table = coef[d, pl.ds(pl.multiple_of(part * vel + row, SUB), SUB), :]

                def load(p, t):
                    return ref[here, p * width + t * LANES : p * width + (t + 1) * LANES]

                def store(p, t, value):
                    swept[d, pl.ds(row, SUB), p * width + t * LANES : p * width + (t + 1) * LANES] = value

                values = sweep_rows(
                    SUB, load, store, table[:, :cells], table[:, cells : 2 * cells], d == 1, pairs, plane
                )
                low = low_half(SUB)
                full, half = packed_last(values, d == 1, whole, low)
                both = jnp.where(low[: SUB // 2], half[: SUB // 2], turn(half[SUB // 2 :]))
                leaving.append((full, both))
            half_row = pl.multiple_of(whole * vel + row // 2, SUB // 2)
            for s in range(1, count):
                forward = (me ^ s) > me
                out = sent[s - 1]
                for w in range(whole):
                    out[pl.ds(pl.multiple_of(w * vel + row, SUB), SUB), :] = jnp.where(
                        forward, leaving[0][0][w], leaving[1][0][w]
                    )
                out[pl.ds(half_row, SUB // 2), :] = jnp.where(forward, leaving[0][1], leaving[1][1])

    pltpu.emit_pipeline(
        body,
        grid=(vel // block,),
        in_specs=[
            pl.BlockSpec((None, block, dist.shape[2]), lambda i: (0, i + offset, 0)),
            pl.BlockSpec((None, block, dist.shape[2]), lambda i: (1, i + offset, 0)),
        ],
    )(dist, dist)
    lane = lax.broadcasted_iota(jnp.int32, (8, LANES), 1)
    passed = []
    for d in range(2):
        last = (cells if d == 1 else 2 * cells - 1)
        tile = jnp.zeros((8, LANES), f32)
        for j in range(vel // 8):
            at = part * vel + 8 * j
            tile = jnp.where(lane == j, jnp.broadcast_to(coef[d, at : at + 8, last : last + 1], (8, LANES)), tile)
        passed.append(tile)
    tail = whole * vel + vel // 2
    for s in range(1, count):
        sent[s - 1][tail : tail + 8, :] = jnp.where((me ^ s) > me, passed[0], passed[1])


def moment_kernel(weight, *refs):
    parts, out = refs[:-1], refs[-1]
    vel, lanes = parts[0].shape[1], parts[0].shape[2]
    chunk = 4 * LANES
    k = out.shape[0]

    @pl.loop(0, lanes // chunk)
    def _(i):
        at = pl.ds(pl.multiple_of(i * chunk, chunk), chunk)
        total = jnp.zeros((k, chunk), f32)
        for d in range(2):
            for c, part in enumerate(parts):
                high, rest = halves(part[d, :, at])
                both = weight[d, :, c * vel : (c + 1) * vel]
                first = dot(both, high)
                total += first[:k] + first[k:] + dot(both[:k], rest)
        out[:, at] = total


def correct_kernel(plane, parts, moments, first_lhs, second_lhs, *refs):
    count = lax.axis_size("gx")
    got = refs[: parts * (count - 1)]
    entering, mine, other, work = refs[parts * (count - 1) :]
    me = lax.axis_index("gx")
    core = lax.axis_index("vert") % 2
    tiles, whole = 2 * plane // LANES, plane // LANES
    vel = entering.shape[1] // parts
    k = moments.shape[0]
    pairs = moments.shape[1] // (2 * plane)
    low = low_half(SUB)
    tail = whole * vel + vel // 2
    for c in range(parts):
        refs_c = got[c * (count - 1) : (c + 1) * (count - 1)]
        passed = [r[tail : tail + 8, :] for r in refs_c]
        scale = []
        for s in range(1, count):
            q = me ^ s
            product = jnp.ones((8, LANES), f32)
            for z in range(1, count):
                if z != s:
                    h = me ^ z
                    between = ((q < h) & (h < me)) | ((me < h) & (h < q))
                    product = product * jnp.where(between, passed[z - 1], 1.0)
            scale.append((jnp.where(q < me, product, 0.0), jnp.where(q > me, product, 0.0)))
        for sub in range(vel // SUB):
            row = sub * SUB
            full = [[jnp.zeros((SUB, LANES), f32)] * whole for _ in range(2)]
            half = [jnp.zeros((SUB, LANES), f32) for _ in range(2)]
            for s in range(1, count):
                ref = refs_c[s - 1]
                packed = ref[whole * vel + row // 2 : whole * vel + (row + SUB) // 2, :]
                ends = jnp.concatenate([packed, turn(packed)], axis=0)
                for d in range(2):
                    by = jnp.concatenate(
                        [
                            jnp.broadcast_to(scale[s - 1][d][:, j : j + 1], (8, LANES))
                            for j in range(row // 8, (row + SUB) // 8)
                        ],
                        axis=0,
                    )
                    full[d] = [full[d][w] + by * ref[w * vel + row : w * vel + row + SUB, :] for w in range(whole)]
                    half[d] = half[d] + by * ends
            for d in range(2):
                cell = full[d] + [half[d]]
                turned = [turn(x) for x in cell]
                pair = full[d] + [jnp.where(low, half[d], turned[0])]
                for w in range(whole):
                    pair.append(jnp.where(low, turned[w], turned[w + 1]))
                for t in range(tiles):
                    entering[d, c * vel + row : c * vel + row + SUB, t * LANES : (t + 1) * LANES] = pair[t]
    width = 2 * plane
    place = lax.broadcasted_iota(jnp.int32, (first_lhs.shape[1] // 3, width), 1)
    total = jnp.zeros(place.shape, f32)
    rows = place.shape[0]
    for d in range(2):
        high, rest = halves(entering[d])
        a, b = first_lhs[d], second_lhs[d]
        even = dot(a[:rows], high) + dot(a[rows : 2 * rows], high) + dot(a[:rows], rest)
        odd = dot(b[:rows], high) + dot(b[rows : 2 * rows], high) + dot(b[:rows], rest)
        total += jnp.where(place < plane, even, odd)
    work[...] = total
    for p in range(pairs):
        at = slice(p * width, (p + 1) * width)
        value = moments[:, at] + work[p * k : (p + 1) * k, :]
        half_pairs = pairs // 2
        inner = slice((p % half_pairs) * width, (p % half_pairs + 1) * width)

        @pl.when(core == p // half_pairs)
        def _():
            mine[:, inner] = value

        @pl.when(core != p // half_pairs)
        def _():
            other[:, inner] = value


def fit_rows(m):
    density = 1.0 + 0.5 * jnp.tanh(m[0:1])
    u = [0.5 * jnp.tanh(m[j : j + 1]) for j in (1, 2, 3)]
    inverse = 1.0 / (1.0 + 0.5 * jnp.tanh(m[4:5]))
    s = [0.2 * jnp.tanh(m[j : j + 1]) for j in range(5, 10)]
    q = [0.2 * jnp.tanh(m[j : j + 1]) for j in range(10, 13)]
    h = 0.5 * inverse
    uu = u[0] * u[0] + u[1] * u[1] + u[2] * u[2]
    qu = q[0] * u[0] + q[1] * u[1] + q[2] * u[2]
    e = h * 1.4426950408889634
    zero = jnp.zeros_like(e)
    exponent = [-e * uu, 2.0 * e * u[0], 2.0 * e * u[1], 2.0 * e * u[2], -e, -e, -e]
    exponent = exponent + [zero] * (16 - len(exponent))
    a = h * uu - 2.5
    xx, yy, zz = 0.5 * s[3], 0.5 * s[4], -0.5 * (s[3] + s[4])
    xy, xz, yz = s[0], s[1], s[2]
    gx = xx * u[0] + 0.5 * (xy * u[1] + xz * u[2])
    gy = yy * u[1] + 0.5 * (xy * u[0] + yz * u[2])
    gz = zz * u[2] + 0.5 * (xz * u[0] + yz * u[1])
    form = gx * u[0] + gy * u[1] + gz * u[2]
    two = 2.0 * h
    scale = density * inverse * jnp.sqrt(inverse)
    by = scale * inverse
    square = qu * h
    terms = [
        scale + by * (form - qu * a),
        by * (a * q[0] + two * qu * u[0] - 2.0 * gx),
        by * (a * q[1] + two * qu * u[1] - 2.0 * gy),
        by * (a * q[2] + two * qu * u[2] - 2.0 * gz),
        by * (xx - two * q[0] * u[0] - square),
        by * (yy - two * q[1] * u[1] - square),
        by * (zz - two * q[2] * u[2] - square),
        by * (xy - two * (q[0] * u[1] + q[1] * u[0])),
        by * (xz - two * (q[0] * u[2] + q[2] * u[0])),
        by * (yz - two * (q[1] * u[2] + q[2] * u[1])),
        by * (h * q[0]),
        by * (h * q[1]),
        by * (h * q[2]),
    ]
    terms = terms + [zero] * (16 - len(terms))
    return jnp.concatenate(exponent, axis=0), jnp.concatenate(terms, axis=0)


def stacked_right(x):
    a, b, c = thirds(x)
    return jnp.concatenate([a, b, a, c, b, a], axis=0)


def stacked_left(x):
    a, b, c = outside_thirds(x)
    return jnp.concatenate([a, a, b, a, b, c], axis=-1)


def finish_kernel(plane, parts, *refs):
    swept = refs[:parts]
    entering, coef, left_e, left_p, mine, other, edge_a, edge_b = refs[parts : parts + 8]
    updated, macro, wide, right_e, right_p = refs[parts + 8 :]
    me, count = lax.axis_index("gx"), lax.axis_size("gx")
    core = lax.axis_index("vert") % 2
    lanes = macro.shape[1]
    cells = lanes // plane
    margin = SMOOTH * plane
    half = lanes // 2
    k = wide.shape[0]
    width = 2 * plane
    pairs = cells // 2

    @pl.when(core == 0)
    def _():
        wide[:, :margin] = edge_b[...]
        wide[:, margin : margin + half] = mine[...]
        wide[:, margin + half : margin + lanes] = other[...]
        wide[:, margin + lanes :] = edge_a[...]

    @pl.when(core != 0)
    def _():
        wide[:, :margin] = edge_a[...]
        wide[:, margin : margin + half] = other[...]
        wide[:, margin + half : margin + lanes] = mine[...]
        wide[:, margin + lanes :] = edge_b[...]

    value = wide[...]
    total = value.shape[1]
    place = lax.broadcasted_iota(jnp.int32, (1, total), 1) + (me * lanes - margin)
    inside = (place >= 0) & (place < count * lanes)
    for _ in range(SMOOTH):
        rate = RATE / (1.0 + value[0:1] * value[0:1])
        rate = jnp.where(inside, rate, 0.0)
        value = value + rate * (pltpu.roll(value, plane, 1) + pltpu.roll(value, total - plane, 1) - 2.0 * value)
    value = value[:, margin : margin + lanes]
    wide[:, :lanes] = value
    macro[...] = value[: macro.shape[0]]

    @pl.loop(0, lanes // (2 * width))
    def _(i):
        at = pl.ds(pl.multiple_of(i * 2 * width, 2 * width), 2 * width)
        exponent, terms = fit_rows(wide[:, at])
        right_e[:, at] = stacked_right(exponent)
        right_p[:, at] = stacked_right(terms)

    vel = swept[0].shape[1]
    block = min(vel, 2 * LANES)
    tiles, whole = 2 * plane // LANES, plane // LANES
    low = low_half(SUB)

    def body(*outs):
        p = pl.program_id(0)
        at = pl.ds(pl.multiple_of(p * width, width), width)
        be, bp = right_e[:, at], right_p[:, at]
        for d in range(2):
            for c in range(parts):
                for row in range(0, vel, block):
                    there = slice(c * vel + row, c * vel + row + block)
                    equil = jnp.exp2(dot(left_e[d, there, :], be)) * dot(left_p[d, there, :], bp)
                    for sub in range(0, block, SUB):
                        line = slice(c * vel + row + sub, c * vel + row + sub + SUB)
                        table = coef[d, line, :]
                        kept = jnp.broadcast_to(table[:, 3 * cells : 3 * cells + 1], (SUB, LANES))
                        table = pltpu.roll(table, 4 * LANES - 2 * cells - 2 * p, 1)
                        first = jnp.broadcast_to(table[:, 0:1], (SUB, LANES))
                        second = jnp.broadcast_to(table[:, 1:2], (SUB, LANES))
                        reach = by_cell(first, second, tiles, whole, low)
                        for t in range(tiles):
                            tile = slice(t * LANES, (t + 1) * LANES)
                            here = pl.ds(pl.multiple_of(p * width + t * LANES, LANES), LANES)
                            outs[d][line, tile] = (
                                kept * swept[c][d, row + sub : row + sub + SUB, here]
                                + reach[t] * entering[d, line, tile]
                                + equil[sub : sub + SUB, tile]
                            )

    spec = lambda d: pl.BlockSpec((None, updated.shape[1], width), lambda i: (d, 0, i))
    pltpu.emit_pipeline(body, grid=(pairs,), out_specs=[spec(0), spec(1)])(updated, updated)


def in_vmem(x):
    return pltpu.with_memory_space_constraint(x, pltpu.VMEM)


def per_device(dist, factors, velocity, weights, relax):
    _, vel, lanes = dist.shape
    cells = factors.shape[2]
    plane = lanes // cells
    count = lax.axis_size("gx")
    moments_n = weights.shape[0]
    k = 16
    pairs = cells // 2
    tiles, whole = 2 * plane // LANES, plane // LANES
    width = 2 * plane
    vel_part = vel // PARTS
    vmem = pl.BlockSpec(memory_space=pltpu.VMEM)
    anywhere = pl.BlockSpec(memory_space=pl.ANY)
    params = lambda mib: pltpu.CompilerParams(vmem_limit_bytes=mib * MIB)

    reach = jnp.stack(
        [jnp.cumprod(factors[0], axis=-1), jnp.cumprod(factors[1][:, ::-1], axis=-1)[:, ::-1]]
    )
    gain = jnp.sqrt(1.0 - factors * factors) / reach
    kept = 1.0 - relax
    coef = jnp.concatenate(
        [gain, reach, reach * kept[..., None], kept[..., None], jnp.zeros((2, vel, LANES - 3 * cells - 1), f32)],
        axis=-1,
    )

    payload = whole * vel_part + vel_part // 2 + 8
    swept, sent = [], []
    for part in range(PARTS):
        out = pl.pallas_call(
            lambda *refs, part=part: sweep_kernel(part, min(SUB, vel_part), plane, *refs),
            out_shape=[pltpu.VMEM((2, vel_part, lanes), f32)]
            + [jax.ShapeDtypeStruct((payload, LANES), f32)] * (count - 1),
            in_specs=[anywhere, vmem],
            out_specs=[vmem] * count,
            compiler_params=params(16),
            name="sweep",
        )(dist, coef)
        swept.append(in_vmem(out[0]))
        sent.append(out[1:])

    got = []
    for part in range(PARTS):
        for s in range(1, count):
            got.append(lax.ppermute(sent[part][s - 1], "gx", [(i, i ^ s) for i in range(count)]))

    padded = jnp.pad(jnp.moveaxis(weights, 1, 0), ((0, 0), (0, k - moments_n), (0, 0)))
    w_high = rounded(padded)
    w_rest = rounded(padded - w_high)
    both = jnp.concatenate([w_high, w_rest], axis=1).astype(bf16)
    moments = pl.pallas_call(
        moment_kernel,
        out_shape=jax.ShapeDtypeStruct((k, lanes), f32),
        in_specs=[vmem] * (1 + PARTS),
        out_specs=vmem,
        compiler_params=params(16),
        name="moments",
    )(both, *swept)

    by_cells = jnp.moveaxis(reach, 2, 1)
    product = by_cells[:, :, None, :] * padded[:, None, :, :]
    product = product.reshape(2, pairs, 2, k, vel)
    product = jnp.moveaxis(product, 2, 0).reshape(2, 2, pairs * k, vel)
    p_high = rounded(product)
    p_rest = rounded(product - p_high)
    lhs = jnp.concatenate([p_high, p_rest, jnp.zeros_like(p_rest)], axis=2).astype(bf16)
    entering, mine, other = pl.pallas_call(
        lambda *refs: correct_kernel(plane, PARTS, *refs),
        out_shape=[
            pltpu.VMEM((2, vel, width), f32),
            jax.ShapeDtypeStruct((k, lanes // 2), f32),
            jax.ShapeDtypeStruct((k, lanes // 2), f32),
        ],
        in_specs=[vmem] * (3 + len(got)),
        out_specs=[vmem] * 3,
        scratch_shapes=[pltpu.VMEM((pairs * k, width), f32)],
        compiler_params=params(24),
        name="correct",
    )(moments, lhs[0], lhs[1], *got)

    size = lax.axis_size("vert")
    core = lax.axis_index("vert") % 2
    total = mine + lax.ppermute(other, "vert", [(i, i ^ 1) for i in range(size)])
    step = 2
    while step < size:
        total = total + lax.ppermute(total, "vert", [(i, i ^ step) for i in range(size)])
        step *= 2
    rest = lax.ppermute(total, "vert", [(i, i ^ 1) for i in range(size)])
    margin = SMOOTH * plane
    edge = jnp.where(core == 0, total[:, :margin], total[:, -margin:])
    near, far = [], []
    for g in range(count):
        for v in range(size):
            to = g - 1 if v % 2 == 0 else g + 1
            if 0 <= to < count:
                near.append((g * size + v, to * size + v))
                far.append((g * size + v, to * size + (v ^ 1)))
    edge_a = lax.ppermute(edge, ("gx", "vert"), near)
    edge_b = lax.ppermute(edge, ("gx", "vert"), far)

    vx, vy, vz = velocity[0], velocity[1], velocity[2]
    xx, yy, zz = vx * vx, vy * vy, vz * vz
    vv = xx + yy + zz
    one = jnp.ones_like(vx)
    zero = jnp.zeros_like(vx)
    base = [one, vx, vy, vz, xx, yy, zz]
    left_e = stacked_left(jnp.stack(base + [zero] * (k - len(base)), axis=-1))
    base = base + [vx * vy, vx * vz, vy * vz, vx * vv, vy * vv, vz * vv]
    left_p = stacked_left(jnp.stack(base + [zero] * (k - len(base)), axis=-1) * relax[..., None])

    depth = left_e.shape[-1]
    updated, macro = pl.pallas_call(
        lambda *refs: finish_kernel(plane, PARTS, *refs),
        out_shape=[jax.ShapeDtypeStruct(dist.shape, f32), jax.ShapeDtypeStruct((moments_n, lanes), f32)],
        in_specs=[vmem] * (PARTS + 8),
        out_specs=[anywhere, vmem],
        scratch_shapes=[
            pltpu.VMEM((k, lanes + 2 * margin), f32),
            pltpu.VMEM((depth, lanes), bf16),
            pltpu.VMEM((depth, lanes), bf16),
        ],
        compiler_params=params(24),
        name="finish",
    )(*swept, in_vmem(entering), coef, left_e, left_p, total, rest, edge_a, edge_b)
    return updated, macro


def solution(mesh):
    return jax.shard_map(
        per_device,
        mesh=mesh,
        in_specs=(
            P(None, "vert", "gx"),
            P(None, "vert", "gx"),
            P(None, None, "vert"),
            P(None, None, "vert"),
            P(None, "vert"),
        ),
        out_specs=(P(None, "vert", "gx"), P(None, "gx")),
        check_vma=False,
    )
```

```python
import jax
import jax.numpy as jnp
from jax import lax
from jax.experimental import pallas as pl
from jax.experimental.pallas import tpu as pltpu
from jax.sharding import PartitionSpec as P

SMOOTH = 4
RATE = 0.24
LANES = 128
PARTS = 2
BLOCK = 128
SUB = 32
ROWS = 64
GROUP = 4
MIB = 2**20

f32 = jnp.float32
bf16 = jnp.bfloat16


def dot(a, b):
    return jnp.dot(a, b, preferred_element_type=f32)


def halves(x):
    high = x.astype(bf16)
    return high, (x - high.astype(f32)).astype(bf16)


def thirds(x):
    high = x.astype(bf16)
    rest = x - high.astype(f32)
    middle = rest.astype(bf16)
    return high, middle, (rest - middle.astype(f32)).astype(bf16)


def low_half(rows):
    return lax.broadcasted_iota(jnp.int32, (rows, LANES), 1) < LANES // 2


def turn(x):
    return pltpu.roll(x, LANES // 2, 1)


def swap_cells(pair, whole, low):
    tiles = len(pair)
    turned = [turn(t) for t in pair]
    return [
        jnp.where(low, turned[(t + whole) % tiles], turned[(t + whole + 1) % tiles])
        for t in range(tiles)
    ]


def seen_before(new, old, backward, whole, low):
    first, second = (old, new) if backward else (new, old)
    return first[:whole] + [jnp.where(low, first[whole], second[whole])] + second[whole + 1 :]


def sweep_rows(rows, load, store, gains, backward, pairs, plane):
    tiles, whole = 2 * plane // LANES, plane // LANES
    low = low_half(rows)
    sums = [jnp.zeros((rows, LANES), f32)] * tiles
    for step in range(pairs):
        p = pairs - 1 - step if backward else step
        gain = gains(p)
        old = sums
        sums = [old[t] + gain[:, t * LANES : (t + 1) * LANES] * load(p, t) for t in range(tiles)]
        for t in range(tiles):
            store(p, t, sums[t])
    crossed = swap_cells(seen_before(sums, old, backward, whole, low), whole, low)
    return [sums[t] + crossed[t] for t in range(tiles)]


def packed_last(values, backward, whole, low):
    tiles = len(values)
    if backward:
        return values[:whole], values[whole]
    turned = [turn(v) for v in values[whole:]]
    full = [jnp.where(low, turned[i], turned[i + 1]) for i in range(whole)]
    return full, turned[whole]


def prepare_kernel(plane, parts, factors, reach, gain, ends, spread):
    cells, vel = factors.shape[1], factors.shape[2]
    depth = spread.shape[0]
    lane = lax.broadcasted_iota(jnp.int32, (8, LANES), 1)
    for d in range(2):
        value = factors[d]
        rows = [value[i : i + 1] for i in range(cells)]
        order = range(cells - 1, -1, -1) if d == 1 else range(cells)
        product = None
        for i in order:
            product = rows[i] if product is None else product * rows[i]
            reach[d, i : i + 1, :] = product
        whole = reach[d]
        gain[d, :, :] = turned_thirds(jnp.sqrt(1.0 - value * value) / whole, depth)
        column = jnp.concatenate([whole[i : i + 1] for i in order][-1:] * 8, axis=0)
        column = column.T
        for c in range(parts):
            tile = jnp.zeros((8, LANES), f32)
            for j in range(vel // parts // 8):
                at = c * (vel // parts) + 8 * j
                tile = jnp.where(lane == j, jnp.broadcast_to(column[at : at + 8, 0:1], (8, LANES)), tile)
            ends[2 * c + d, :, :] = tile
    row = lax.broadcasted_iota(jnp.int32, (cells, 4 * LANES), 0) * plane
    for at in range(0, spread.shape[1], 4 * LANES):
        place = lax.broadcasted_iota(jnp.int32, (cells, 4 * LANES), 1) + at
        own = jnp.where((place >= row) & (place < row + plane), 1.0, 0.0).astype(bf16)
        for i in range(3):
            spread[i * cells : (i + 1) * cells, at : at + 4 * LANES] = own
        if depth > 3 * cells:
            spread[3 * cells :, at : at + 4 * LANES] = jnp.zeros((depth - 3 * cells, 4 * LANES), bf16)


def turned_thirds(x, depth):
    terms = [t.astype(f32) for t in thirds(x)]
    rest = depth - 3 * x.shape[0]
    if rest:
        terms.append(jnp.zeros((rest, x.shape[1]), f32))
    return jnp.concatenate(terms, axis=0).T.astype(bf16)


def sweep_kernel(part, rows, plane, dist, gain, ends, spread, *rest):
    swept, sent = rest[0], rest[1:]
    count = len(sent) + 1
    me = lax.axis_index("gx")
    vel = swept.shape[1]
    pairs = swept.shape[2] // plane // 2
    whole = plane // LANES
    width = 2 * plane
    offset = part * (vel // rows)
    low = low_half(rows)
    some = min(ROWS, rows)

    def body(ref):
        step = pl.program_id(0)
        row = pl.multiple_of(step // 2 * rows, rows)

        def one(d):
            table = gain[d, pl.ds(pl.multiple_of(part * vel + row, rows), rows), :]

            def gains(p):
                return dot(table, spread[:, p * width : (p + 1) * width])

            def load(p, t):
                return ref[:, p * width + t * LANES : p * width + (t + 1) * LANES]

            def store(p, t, value):
                swept[d, pl.ds(row, rows), p * width + t * LANES : p * width + (t + 1) * LANES] = value

            values = sweep_rows(rows, load, store, gains, d == 1, pairs, plane)
            full, half = packed_last(values, d == 1, whole, low)
            both = [
                jnp.where(low[: some // 2], half[n : n + some // 2], turn(half[n + some // 2 : n + some]))
                for n in range(0, rows, some)
            ]
            for s in range(1, count):
                out = sent[s - 1]

                @pl.when(((me ^ s) > me) == (d == 0))
                def _():
                    for w in range(whole):
                        out[pl.ds(pl.multiple_of(w * vel + row, rows), rows), :] = full[w]
                    for n, packed in enumerate(both):
                        out[pl.ds(pl.multiple_of(whole * vel + (row + n * some) // 2, some // 2), some // 2), :] = packed

        for d in range(2):
            pl.when(step % 2 == d)(lambda d=d: one(d))

    pltpu.emit_pipeline(
        body,
        grid=(2 * vel // rows,),
        in_specs=[
            pl.BlockSpec(
                (None, rows, dist.shape[2]), lambda i: (i % 2, i // 2 + offset, 0), pipeline_mode=pl.Buffered(3)
            )
        ],
    )(dist)
    tail = whole * vel + vel // 2
    for s in range(1, count):
        sent[s - 1][tail : tail + 8, :] = jnp.where((me ^ s) > me, ends[2 * part], ends[2 * part + 1])


def moment_kernel(plane, parts, reach, weight, *refs):
    sums = refs[:parts]
    out, high_lhs, rest_lhs, next_high, next_rest = refs[parts:]
    vel = sums[0].shape[1]
    k = weight.shape[1]
    width = 2 * plane
    pairs = next_high.shape[1] // k
    whole = plane // LANES
    low = low_half(k)
    for d in range(2):
        for p in range(pairs):
            rows = [weight[d] * reach[d, 2 * p : 2 * p + 1, :], weight[d] * reach[d, 2 * p + 1 : 2 * p + 2, :]]
            both = slice(2 * p * k, 2 * (p + 1) * k)
            high_lhs[d, both, :], rest_lhs[d, both, :] = halves(jnp.concatenate(rows, axis=0))
            q = p + 1 if d == 1 else p - 1
            if 0 <= q < pairs:
                at = slice(q * k, (q + 1) * k)
                next_high[d, at, :], next_rest[d, at, :] = halves(rows[d])
        q = 0 if d == 1 else pairs - 1
        at = slice(q * k, (q + 1) * k)
        next_high[d, at, :] = jnp.zeros((k, weight.shape[2]), bf16)
        next_rest[d, at, :] = jnp.zeros((k, weight.shape[2]), bf16)
    first = lax.broadcasted_iota(jnp.int32, (k, width), 1) < plane
    out[...] = jnp.zeros(out.shape, f32)

    def exchanged(x):
        tiles = [x[:, t : t + LANES] for t in range(0, width, LANES)]
        return jnp.concatenate(swap_cells(tiles, whole, low), axis=1)

    @pl.loop(0, pairs)
    def _(p):
        at = pl.ds(pl.multiple_of(p * width, width), width)
        ahead = jnp.minimum(p + 1, pairs - 1)
        behind = jnp.maximum(p - 1, 0)
        here = jnp.zeros((k, width), f32)
        for d in range(2):
            total = jnp.zeros((3 * k, width), f32)
            for c, part in enumerate(sums):
                high, rest = halves(part[d, :, at])
                cols = slice(c * vel, (c + 1) * vel)
                own = pl.ds(pl.multiple_of(p * 2 * k, 2 * k), 2 * k)
                after = pl.ds(pl.multiple_of(p * k, k), k)
                left = [high_lhs[d, own, cols], next_high[d, after, cols], rest_lhs[d, own, cols], next_rest[d, after, cols]]
                main = dot(jnp.concatenate(left, axis=0), high)
                total += main[: 3 * k] + main[3 * k :] + dot(jnp.concatenate(left[:2], axis=0), rest)
            even, odd, after = total[:k], total[k : 2 * k], total[2 * k :]
            if d == 0:
                here += jnp.where(first, even, odd + exchanged(odd))
                moved = jnp.where(first, exchanged(after), 0.0)
                out[:, pl.ds(pl.multiple_of(ahead * width, width), width)] += moved
            else:
                here += jnp.where(first, even + exchanged(even), odd)
                moved = jnp.where(first, 0.0, exchanged(after))
                out[:, pl.ds(pl.multiple_of(behind * width, width), width)] += moved
        out[:, at] += here


def correct_kernel(plane, part, last, moments, high_lhs, rest_lhs, *refs):
    count = lax.axis_size("gx")
    refs_c, refs = refs[: count - 1], refs[count - 1 :]
    entering, outs, (natural, work) = refs[0], refs[1:-2], refs[-2:]
    me = lax.axis_index("gx")
    core = lax.axis_index("vert") % 2
    tiles, whole = 2 * plane // LANES, plane // LANES
    vel = entering.shape[1]
    k = moments.shape[0]
    pairs = moments.shape[1] // (2 * plane)
    rows = min(ROWS, vel)
    low = low_half(rows)
    tail = whole * vel + vel // 2
    passed = [r[tail : tail + 8, :] for r in refs_c]
    scale = []
    for s in range(1, count):
        q = me ^ s
        product = jnp.ones((8, LANES), f32)
        for z in range(1, count):
            if z != s:
                h = me ^ z
                between = ((q < h) & (h < me)) | ((me < h) & (h < q))
                product = product * jnp.where(between, passed[z - 1], 1.0)
        product = product * passed[s - 1]
        scale.append((jnp.where(q < me, product, 0.0), jnp.where(q > me, product, 0.0)))
    for sub in range(vel // rows):
        row = sub * rows
        full = [[jnp.zeros((rows, LANES), f32)] * whole for _ in range(2)]
        half = [jnp.zeros((rows, LANES), f32) for _ in range(2)]
        for s in range(1, count):
            ref = refs_c[s - 1]
            packed = ref[whole * vel + row // 2 : whole * vel + (row + rows) // 2, :]
            ends = jnp.concatenate([packed, turn(packed)], axis=0)
            for d in range(2):
                by = jnp.concatenate(
                    [
                        jnp.broadcast_to(scale[s - 1][d][:, j : j + 1], (8, LANES))
                        for j in range(row // 8, (row + rows) // 8)
                    ],
                    axis=0,
                )
                full[d] = [full[d][w] + by * ref[w * vel + row : w * vel + row + rows, :] for w in range(whole)]
                half[d] = half[d] + by * ends
        for d in range(2):
            cell = full[d] + [half[d]]
            for t in range(whole + 1):
                natural[d, row : row + rows, t * LANES : (t + 1) * LANES] = cell[t]
            turned = [turn(x) for x in cell]
            pair = full[d] + [jnp.where(low, half[d], turned[0])]
            for w in range(whole):
                pair.append(jnp.where(low, turned[w], turned[w + 1]))
            for t in range(tiles):
                entering[d, row : row + rows, t * LANES : (t + 1) * LANES] = pair[t]
    low = low_half(k)
    cols = slice(part * vel, (part + 1) * vel)
    for d in range(2):
        high, rest = halves(natural[d])
        total = dot(high_lhs[d, :, cols], high) + dot(rest_lhs[d, :, cols], high) + dot(high_lhs[d, :, cols], rest)
        if d == 0:
            work[...] = total
        else:
            work[...] += total
    half_pairs = pairs // 2
    width = 2 * plane
    for p in range(pairs):
        first, second = ([work[(2 * p + i) * k : (2 * p + i + 1) * k, t : t + LANES] for t in range(0, (whole + 1) * LANES, LANES)] for i in range(2))
        turned = [turn(x) for x in second]
        term = first[:whole] + [jnp.where(low, first[whole], turned[0])]
        term += [jnp.where(low, turned[w], turned[w + 1]) for w in range(whole)]
        value = moments[:, p * width : (p + 1) * width] + jnp.concatenate(term, axis=1)
        if not last:
            outs[0][:, p * width : (p + 1) * width] = value
            continue
        mine, other = outs
        inner = slice((p % half_pairs) * width, (p % half_pairs + 1) * width)

        @pl.when(core == p // half_pairs)
        def _():
            mine[:, inner] = value

        @pl.when(core != p // half_pairs)
        def _():
            other[:, inner] = value


def fit_rows(m):
    density = 1.0 + 0.5 * jnp.tanh(m[0:1])
    u = [0.5 * jnp.tanh(m[j : j + 1]) for j in (1, 2, 3)]
    inverse = 1.0 / (1.0 + 0.5 * jnp.tanh(m[4:5]))
    s = [0.2 * jnp.tanh(m[j : j + 1]) for j in range(5, 10)]
    q = [0.2 * jnp.tanh(m[j : j + 1]) for j in range(10, 13)]
    h = 0.5 * inverse
    uu = u[0] * u[0] + u[1] * u[1] + u[2] * u[2]
    qu = q[0] * u[0] + q[1] * u[1] + q[2] * u[2]
    e = h * 1.4426950408889634
    zero = jnp.zeros_like(e)
    exponent = [-e * uu, 2.0 * e * u[0], 2.0 * e * u[1], 2.0 * e * u[2], -e, -e, -e]
    exponent = exponent + [zero] * (16 - len(exponent))
    a = h * uu - 2.5
    xx, yy, zz = 0.5 * s[3], 0.5 * s[4], -0.5 * (s[3] + s[4])
    xy, xz, yz = s[0], s[1], s[2]
    gx = xx * u[0] + 0.5 * (xy * u[1] + xz * u[2])
    gy = yy * u[1] + 0.5 * (xy * u[0] + yz * u[2])
    gz = zz * u[2] + 0.5 * (xz * u[0] + yz * u[1])
    form = gx * u[0] + gy * u[1] + gz * u[2]
    two = 2.0 * h
    scale = density * inverse * jnp.sqrt(inverse)
    by = scale * inverse
    square = qu * h
    terms = [
        scale + by * (form - qu * a),
        by * (a * q[0] + two * qu * u[0] - 2.0 * gx),
        by * (a * q[1] + two * qu * u[1] - 2.0 * gy),
        by * (a * q[2] + two * qu * u[2] - 2.0 * gz),
        by * (xx - two * q[0] * u[0] - square),
        by * (yy - two * q[1] * u[1] - square),
        by * (zz - two * q[2] * u[2] - square),
        by * (xy - two * (q[0] * u[1] + q[1] * u[0])),
        by * (xz - two * (q[0] * u[2] + q[2] * u[0])),
        by * (yz - two * (q[1] * u[2] + q[2] * u[1])),
        by * (h * q[0]),
        by * (h * q[1]),
        by * (h * q[2]),
    ]
    terms = terms + [zero] * (16 - len(terms))
    return jnp.concatenate(exponent, axis=0), jnp.concatenate(terms, axis=0)


def stacked_right(x):
    a, b, c = thirds(x)
    return jnp.concatenate([a, b, a, c, b, a, jnp.zeros((LANES - 96, x.shape[1]), bf16)], axis=0)


def table_kernel(velocity, relax, reach, _, left_e, left_p, left_r):
    for d in range(2):
        fraction = relax[d]
        x, y, z = (velocity[j, d] for j in range(3))
        xx, yy, zz = x * x, y * y, z * z
        square = xx + yy + zz
        rows = [jnp.ones_like(x), x, y, z, xx, yy, zz, x * y, x * z, y * z, x * square, y * square, z * square]
        rows = jnp.concatenate(rows + [jnp.zeros_like(x)] * (16 - len(rows)), axis=0)
        for ref, value in ((left_e, rows), (left_p, rows * fraction)):
            a, b, c = (t.astype(f32) for t in thirds(value))
            stack = [a, a, b, a, b, c]
            rest = ref.shape[2] - 16 * len(stack)
            if rest:
                stack.append(jnp.zeros((rest, value.shape[1]), f32))
            ref[d, :, :] = jnp.concatenate(stack, axis=0).T.astype(bf16)
        left_r[d, :, :] = turned_thirds(reach[d] * (1.0 - fraction), left_r.shape[2])


def fit_kernel(plane, own, rest, macro, right_e, right_p, wide):
    me, count = lax.axis_index("gx"), lax.axis_size("gx")
    core = lax.axis_index("vert") % 2
    lanes = macro.shape[1]
    cells = lanes // plane
    margin = SMOOTH * plane
    half = lanes // 2
    width = 2 * plane

    for first, left, right in ((0, own, rest), (1, rest, own)):

        @pl.when(core == first)
        def _():
            wide[:, :margin] = left[:, half:]
            wide[:, margin : margin + half] = left[:, :half]
            wide[:, margin + half : margin + lanes] = right[:, :half]
            wide[:, margin + lanes :] = right[:, half:]

    value = wide[...]
    total = value.shape[1]
    place = lax.broadcasted_iota(jnp.int32, (1, total), 1) + (me * lanes - margin)
    inside = (place >= 0) & (place < count * lanes)
    for _ in range(SMOOTH):
        rate = RATE / (1.0 + value[0:1] * value[0:1])
        rate = jnp.where(inside, rate, 0.0)
        value = value + rate * (pltpu.roll(value, plane, 1) + pltpu.roll(value, total - plane, 1) - 2.0 * value)
    value = value[:, margin : margin + lanes]
    wide[:, :lanes] = value
    macro[...] = value[: macro.shape[0]]

    @pl.loop(0, lanes // (2 * width))
    def _(i):
        at = pl.ds(pl.multiple_of(i * 2 * width, 2 * width), 2 * width)
        exponent, terms = fit_rows(wide[:, at])
        right_e[:, at] = stacked_right(exponent)
        right_p[:, at] = stacked_right(terms)


def join_kernel(plane, d, offset, sums, entering, left, spread, _, kept):
    vel = sums.shape[1]
    width = 2 * plane
    tiles, whole = width // LANES, plane // LANES
    pairs = sums.shape[2] // width
    rows = min(ROWS, vel)
    low = low_half(rows)

    def pair(i):
        p = i if d == 1 else pairs - 1 - i
        before = jnp.minimum(p + 1, pairs - 1) if d == 1 else jnp.maximum(p - 1, 0)
        there = jnp.where(i == pairs - 1, 0.0, 1.0)
        place = lambda q, t: pl.ds(pl.multiple_of(q * width + t * LANES, LANES), LANES)
        crossed = []
        for row in range(0, vel, rows):
            line = slice(row, row + rows)
            own = [sums[d, line, place(p, t)] for t in range(tiles)]
            past = [
                None if (t < whole) != (d == 1) and t != whole else there * sums[d, line, place(before, t)]
                for t in range(tiles)
            ]
            crossed.append(swap_cells(seen_before(own, past, d == 1, whole, low), whole, low))
        right = spread[:, pl.ds(pl.multiple_of(p * width, width), width)]
        reach = dot(left[d, offset : offset + vel, :], right)
        for n, row in enumerate(range(0, vel, rows)):
            line = slice(row, row + rows)
            for t in range(tiles):
                tile = slice(t * LANES, (t + 1) * LANES)
                value = sums[d, line, place(p, t)] + crossed[n][t] + entering[d, line, tile]
                kept[d, line, place(p, t)] = reach[line, tile] * value

    @pl.loop(0, pairs // GROUP)
    def _(i):
        for u in range(GROUP):
            pair(i * GROUP + u)


def edge_of(x, width):
    return jnp.where(lax.axis_index("vert") % 2 == 0, x[:, :width], x[:, x.shape[1] - width :])


def add_kernel(a, b, *refs):
    out = refs[-1]
    out[...] = a[...] + b[...]


def edge_kernel(a, b, *refs):
    out, edge = refs[-2:]
    out[...] = a[...] + b[...]
    edge[...] = edge_of(out, edge.shape[1])


def close_kernel(a, b, halo, more, *refs):
    out, lanes = refs[-1], a.shape[1]
    out[:, :lanes] = a[...] + b[...]
    out[:, lanes:] = halo[...] + more[...]


def finish_kernel(plane, parts, *refs):
    kept = refs[:parts]
    left_e, left_p, right_e, right_p, updated = refs[parts:]
    vel = kept[0].shape[1]
    width = 4 * plane
    block = min(vel, BLOCK)

    def body(*outs):
        at = pl.ds(pl.multiple_of(pl.program_id(0) * width, width), width)
        be, bp = right_e[:, at], right_p[:, at]
        for d in range(2):
            for c in range(parts):
                for row in range(0, vel, block):
                    there = slice(c * vel + row, c * vel + row + block)
                    equil = jnp.exp2(dot(left_e[d, there, :], be)) * dot(left_p[d, there, :], bp)
                    outs[d][there, :] = kept[c][d, row : row + block, at] + equil

    spec = lambda d: pl.BlockSpec((None, updated.shape[1], width), lambda i: (d, 0, i))
    pltpu.emit_pipeline(body, grid=(updated.shape[2] // width,), out_specs=[spec(0), spec(1)])(updated, updated)


def in_vmem(x):
    return pltpu.with_memory_space_constraint(x, pltpu.VMEM)


def per_device(dist, factors, velocity, weights, relax):
    _, vel, lanes = dist.shape
    cells = factors.shape[2]
    plane = lanes // cells
    count = lax.axis_size("gx")
    moments_n = weights.shape[0]
    k = 16
    pairs = cells // 2
    tiles, whole = 2 * plane // LANES, plane // LANES
    width = 2 * plane
    vel_part = vel // PARTS
    vmem = pl.BlockSpec(memory_space=pltpu.VMEM)
    anywhere = pl.BlockSpec(memory_space=pl.ANY)
    params = pltpu.CompilerParams(vmem_limit_bytes=12 * MIB)

    depth = -(-3 * cells // LANES) * LANES
    reach, gain, ends, spread = pl.pallas_call(
        lambda *refs: prepare_kernel(plane, PARTS, *refs),
        out_shape=[
            jax.ShapeDtypeStruct((2, cells, vel), f32),
            pltpu.VMEM((2, vel, depth), bf16),
            pltpu.VMEM((2 * PARTS, 8, LANES), f32),
            pltpu.VMEM((depth, lanes), bf16),
        ],
        in_specs=[vmem],
        out_specs=[vmem] * 4,
        compiler_params=params,
        name="prepare",
    )(jnp.swapaxes(factors, 1, 2))
    gain, ends, spread = in_vmem(gain), in_vmem(ends), in_vmem(spread)
    dist = pltpu.with_memory_space_constraint(dist, pltpu.HBM)

    payload = whole * vel_part + vel_part // 2 + 8
    swept, sent = [], []
    for part in range(PARTS):
        out = pl.pallas_call(
            lambda *refs, part=part: sweep_kernel(part, min(BLOCK, vel_part), plane, *refs),
            out_shape=[pltpu.VMEM((2, vel_part, lanes), f32)]
            + [jax.ShapeDtypeStruct((payload, LANES), f32)] * (count - 1),
            in_specs=[pl.BlockSpec(memory_space=pltpu.HBM), vmem, vmem, vmem],
            out_specs=[vmem] * count,
            compiler_params=params,
            name="sweep",
        )(dist, gain, ends, spread)
        swept.append(in_vmem(out[0]))
        sent.append(out[1:])

    padded = jnp.pad(jnp.moveaxis(weights, 1, 0), ((0, 0), (0, k - moments_n), (0, 0)))
    moments, *lhs = pl.pallas_call(
        lambda *refs: moment_kernel(plane, PARTS, *refs),
        out_shape=[jax.ShapeDtypeStruct((k, lanes), f32)]
        + [pltpu.VMEM((2, 2 * pairs * k, vel), bf16)] * 2,
        in_specs=[vmem] * (2 + PARTS),
        out_specs=[vmem] * 3,
        scratch_shapes=[pltpu.VMEM((2, pairs * k, vel), bf16)] * 2,
        compiler_params=params,
        name="moments",
    )(reach, padded, *swept)

    left_e, left_p, left_r = pl.pallas_call(
        table_kernel,
        out_shape=[pltpu.VMEM((2, vel, LANES), bf16)] * 2 + [pltpu.VMEM((2, vel, depth), bf16)],
        in_specs=[vmem] * 3 + [anywhere],
        out_specs=[vmem] * 3,
        compiler_params=params,
        name="tables",
    )(velocity[:, :, None, :], relax[:, None, :], reach, moments)

    entering = []
    for part in range(PARTS):
        last = part == PARTS - 1
        got = [
            lax.ppermute(sent[part][s - 1], "gx", [(i, i ^ s) for i in range(count)]) for s in range(1, count)
        ]
        out = [jax.ShapeDtypeStruct((k, lanes // 2), f32)] * 2 if last else [jax.ShapeDtypeStruct((k, lanes), f32)]
        found, *moments = pl.pallas_call(
            lambda *refs, part=part, last=last: correct_kernel(plane, part, last, *refs),
            out_shape=[pltpu.VMEM((2, vel_part, width), f32)] + out,
            in_specs=[vmem] * (3 + len(got)),
            out_specs=[vmem] * (1 + len(out)),
            scratch_shapes=[
                pltpu.VMEM((2, vel_part, (whole + 1) * LANES), f32),
                pltpu.VMEM((2 * pairs * k, (whole + 1) * LANES), f32),
            ],
            compiler_params=params,
            name="correct",
        )(*(moments if part else [moments]), *[in_vmem(x) for x in lhs], *got)
        entering.append(in_vmem(found))
    mine, other = moments

    size = lax.axis_size("vert")
    margin = SMOOTH * plane
    half = (k, lanes // 2)
    kept = list(swept)

    def join(part, d, after):
        kept[part] = pl.pallas_call(
            lambda *refs: join_kernel(plane, d, part * vel_part, *refs),
            out_shape=pltpu.VMEM(kept[part].shape, f32),
            in_specs=[vmem] * 4 + [anywhere],
            out_specs=vmem,
            input_output_aliases={0: 0},
            compiler_params=params,
            cost_estimate=pl.CostEstimate(
                flops=4 * dist.size * LANES // (2 * PARTS), bytes_accessed=4 * dist.size // PARTS, transcendentals=0
            ),
            name="join",
        )(in_vmem(kept[part]), entering[part], in_vmem(left_r), spread, after)
        return in_vmem(kept[part])

    def combine(kernel, out, *args):
        done = [x for x in args if x is not None]
        return pl.pallas_call(
            kernel,
            out_shape=[jax.ShapeDtypeStruct(x, f32) for x in out],
            in_specs=[vmem] * len(done),
            out_specs=[vmem] * len(out),
            compiler_params=params,
            name=kernel.__name__,
        )(*done)

    steps = [1]
    while 2 * steps[-1] < size:
        steps.append(2 * steps[-1])
    total, beside = mine, None
    chunks = [(part, d) for part in range(PARTS) for d in range(2)]
    for i, step in enumerate(steps[:-1]):
        got = lax.ppermute(total if i else other, "vert", [(v, v ^ step) for v in range(size)])
        if i:
            beside = join(*chunks.pop(0), total) if len(chunks) > 3 else None
        if i == len(steps) - 2:
            total, edge = combine(edge_kernel, [half, (k, margin)], total, got, beside)
        else:
            (total,) = combine(add_kernel, [half], total, got, beside)
    step = steps[-1]
    got = lax.ppermute(total, "vert", [(v, v ^ step) for v in range(size)])
    beyond = []
    for g in range(count - 1):
        for v in range(1, size, 2):
            near, far = g * size + v, (g + 1) * size + v - 1
            beyond += [(near, far), (far, near)]
    halo = lax.ppermute(edge, ("gx", "vert"), beyond)
    join(*chunks.pop(0), total)
    more = lax.ppermute(halo, "vert", [(v, v ^ step) for v in range(size)])
    while chunks:
        join(*chunks.pop(0), halo)
    (own,) = combine(close_kernel, [(k, lanes // 2 + margin)], total, got, halo, more, *[in_vmem(x) for x in kept])
    rest = lax.ppermute(own, "vert", [(v, v ^ 1) for v in range(size)])

    macro, right_e, right_p = pl.pallas_call(
        lambda *refs: fit_kernel(plane, *refs),
        out_shape=[jax.ShapeDtypeStruct((moments_n, lanes), f32)] + [pltpu.VMEM((LANES, lanes), bf16)] * 2,
        in_specs=[vmem] * 2,
        out_specs=[vmem] * 3,
        scratch_shapes=[pltpu.VMEM((k, lanes + 2 * margin), f32)],
        compiler_params=params,
        name="fit",
    )(own, rest)

    last = [*kept, left_e, left_p, right_e, right_p]
    updated = pl.pallas_call(
        lambda *refs: finish_kernel(plane, PARTS, *refs),
        out_shape=jax.ShapeDtypeStruct(dist.shape, f32),
        in_specs=[vmem] * len(last),
        out_specs=anywhere,
        compiler_params=params,
        name="finish",
    )(*[in_vmem(x) for x in last])
    return updated, macro


def solution(mesh):
    return jax.shard_map(
        per_device,
        mesh=mesh,
        in_specs=(
            P(None, "vert", "gx"),
            P(None, "vert", "gx"),
            P(None, None, "vert"),
            P(None, None, "vert"),
            P(None, "vert"),
        ),
        out_specs=(P(None, "vert", "gx"), P(None, "gx")),
        check_vma=False,
    )
```

```python
import jax
import jax.numpy as jnp
from jax import lax
from jax.experimental import pallas as pl
from jax.experimental.pallas import tpu as pltpu
from jax.sharding import PartitionSpec as P

SMOOTH = 4
RATE = 0.24
LANES = 128
PARTS = 2
BLOCK = 128
SUB = 32
ROWS = 64
GROUP = 4
MIB = 2**20

f32 = jnp.float32
bf16 = jnp.bfloat16


def dot(a, b):
    return jnp.dot(a, b, preferred_element_type=f32)


def halves(x):
    high = x.astype(bf16)
    return high, (x - high.astype(f32)).astype(bf16)


def thirds(x):
    high = x.astype(bf16)
    rest = x - high.astype(f32)
    middle = rest.astype(bf16)
    return high, middle, (rest - middle.astype(f32)).astype(bf16)


def low_half(rows):
    return lax.broadcasted_iota(jnp.int32, (rows, LANES), 1) < LANES // 2


def turn(x):
    return pltpu.roll(x, LANES // 2, 1)


def swap_cells(pair, whole, low):
    tiles = len(pair)
    turned = [turn(t) for t in pair]
    return [
        jnp.where(low, turned[(t + whole) % tiles], turned[(t + whole + 1) % tiles])
        for t in range(tiles)
    ]


def seen_before(new, old, backward, whole, low):
    first, second = (old, new) if backward else (new, old)
    return first[:whole] + [jnp.where(low, first[whole], second[whole])] + second[whole + 1 :]


def sweep_rows(rows, load, store, gains, backward, pairs, plane):
    tiles, whole = 2 * plane // LANES, plane // LANES
    low = low_half(rows)
    sums = [jnp.zeros((rows, LANES), f32)] * tiles
    for step in range(pairs):
        p = pairs - 1 - step if backward else step
        gain = gains(p)
        old = sums
        sums = [old[t] + gain[:, t * LANES : (t + 1) * LANES] * load(p, t) for t in range(tiles)]
        for t in range(tiles):
            store(p, t, sums[t])
    crossed = swap_cells(seen_before(sums, old, backward, whole, low), whole, low)
    return [sums[t] + crossed[t] for t in range(tiles)]


def packed_last(values, backward, whole, low):
    tiles = len(values)
    if backward:
        return values[:whole], values[whole]
    turned = [turn(v) for v in values[whole:]]
    full = [jnp.where(low, turned[i], turned[i + 1]) for i in range(whole)]
    return full, turned[whole]


def prepare(plane, parts, factors, reach, gain, ends, spread):
    cells, vel = factors.shape[1], factors.shape[2]
    depth = spread.shape[0]
    lane = lax.broadcasted_iota(jnp.int32, (8, LANES), 1)
    for d in range(2):
        value = factors[d]
        rows = [value[i : i + 1] for i in range(cells)]
        order = range(cells - 1, -1, -1) if d == 1 else range(cells)
        product = None
        for i in order:
            product = rows[i] if product is None else product * rows[i]
            reach[d, i : i + 1, :] = product
        whole = reach[d]
        gain[d, :, :] = turned_thirds(jnp.sqrt(1.0 - value * value) / whole, depth)
        column = jnp.concatenate([whole[i : i + 1] for i in order][-1:] * 8, axis=0)
        column = column.T
        for c in range(parts):
            tile = jnp.zeros((8, LANES), f32)
            for j in range(vel // parts // 8):
                at = c * (vel // parts) + 8 * j
                tile = jnp.where(lane == j, jnp.broadcast_to(column[at : at + 8, 0:1], (8, LANES)), tile)
            ends[2 * c + d, :, :] = tile
    row = lax.broadcasted_iota(jnp.int32, (cells, 4 * LANES), 0) * plane
    for at in range(0, spread.shape[1], 4 * LANES):
        place = lax.broadcasted_iota(jnp.int32, (cells, 4 * LANES), 1) + at
        own = jnp.where((place >= row) & (place < row + plane), 1.0, 0.0).astype(bf16)
        for i in range(3):
            spread[i * cells : (i + 1) * cells, at : at + 4 * LANES] = own
        if depth > 3 * cells:
            spread[3 * cells :, at : at + 4 * LANES] = jnp.zeros((depth - 3 * cells, 4 * LANES), bf16)


def turned_thirds(x, depth):
    terms = [t.astype(f32) for t in thirds(x)]
    rest = depth - 3 * x.shape[0]
    if rest:
        terms.append(jnp.zeros((rest, x.shape[1]), f32))
    return jnp.concatenate(terms, axis=0).T.astype(bf16)


def sweep_kernel(part, rows, plane, parts, count, *refs):
    if part == 0:
        dist, factors, swept, *sent = refs[: 2 + count]
        reach, gain, ends, spread, blocks, arrived, table, read = refs[2 + count :]
    else:
        dist, gain, ends, spread, swept, *sent = refs[: 4 + count]
        blocks, arrived = refs[4 + count :]
    me = lax.axis_index("gx")
    vel = swept.shape[1]
    pairs = swept.shape[2] // plane // 2
    whole = plane // LANES
    width = 2 * plane
    low = low_half(rows)
    some = min(ROWS, rows)
    steps = [(d, row) for row in range(0, vel, rows) for d in range(2)]
    slots = blocks.shape[0]

    def fetch(i):
        d, row = steps[i]
        at = part * vel + row
        return pltpu.make_async_copy(dist.at[d, at : at + rows, :], blocks.at[i % slots], arrived.at[i % slots])

    if part == 0:
        first = pltpu.make_async_copy(factors, table, read)
        first.start()
    for i in range(min(slots, len(steps))):
        fetch(i).start()
    if part == 0:
        first.wait()
        prepare(plane, parts, table, reach, gain, ends, spread)

    for i, (d, row) in enumerate(steps):
        fetch(i).wait()
        ref = blocks.at[i % slots]
        left = gain[d, part * vel + row : part * vel + row + rows, :]

        def gains(p):
            return dot(left, spread[:, p * width : (p + 1) * width])

        def load(p, t):
            return ref[:, p * width + t * LANES : p * width + (t + 1) * LANES]

        def store(p, t, value):
            swept[d, row : row + rows, p * width + t * LANES : p * width + (t + 1) * LANES] = value

        values = sweep_rows(rows, load, store, gains, d == 1, pairs, plane)
        if i + slots < len(steps):
            fetch(i + slots).start()
        full, half = packed_last(values, d == 1, whole, low)
        both = [
            jnp.where(low[: some // 2], half[n : n + some // 2], turn(half[n + some // 2 : n + some]))
            for n in range(0, rows, some)
        ]
        for s in range(1, count):
            out = sent[s - 1]

            @pl.when(((me ^ s) > me) == (d == 0))
            def _():
                for w in range(whole):
                    out[w * vel + row : w * vel + row + rows, :] = full[w]
                for n, packed in enumerate(both):
                    at = whole * vel + (row + n * some) // 2
                    out[at : at + some // 2, :] = packed

    tail = whole * vel + vel // 2
    for s in range(1, count):
        sent[s - 1][tail : tail + 8, :] = jnp.where((me ^ s) > me, ends[2 * part], ends[2 * part + 1])


def moment_kernel(plane, parts, reach, weight, *refs):
    sums = refs[:parts]
    out, high_lhs, rest_lhs, next_high, next_rest = refs[parts:]
    vel = sums[0].shape[1]
    k = weight.shape[1]
    width = 2 * plane
    pairs = next_high.shape[1] // k
    whole = plane // LANES
    low = low_half(k)
    for d in range(2):
        for p in range(pairs):
            rows = [weight[d] * reach[d, 2 * p : 2 * p + 1, :], weight[d] * reach[d, 2 * p + 1 : 2 * p + 2, :]]
            both = slice(2 * p * k, 2 * (p + 1) * k)
            high_lhs[d, both, :], rest_lhs[d, both, :] = halves(jnp.concatenate(rows, axis=0))
            q = p + 1 if d == 1 else p - 1
            if 0 <= q < pairs:
                at = slice(q * k, (q + 1) * k)
                next_high[d, at, :], next_rest[d, at, :] = halves(rows[d])
        q = 0 if d == 1 else pairs - 1
        at = slice(q * k, (q + 1) * k)
        next_high[d, at, :] = jnp.zeros((k, weight.shape[2]), bf16)
        next_rest[d, at, :] = jnp.zeros((k, weight.shape[2]), bf16)
    first = lax.broadcasted_iota(jnp.int32, (k, width), 1) < plane
    out[...] = jnp.zeros(out.shape, f32)

    def exchanged(x):
        tiles = [x[:, t : t + LANES] for t in range(0, width, LANES)]
        return jnp.concatenate(swap_cells(tiles, whole, low), axis=1)

    def pair(p):
        at = pl.ds(pl.multiple_of(p * width, width), width)
        ahead = jnp.minimum(p + 1, pairs - 1)
        behind = jnp.maximum(p - 1, 0)
        here = jnp.zeros((k, width), f32)
        for d in range(2):
            total = jnp.zeros((3 * k, width), f32)
            for c, part in enumerate(sums):
                high, rest = halves(part[d, :, at])
                cols = slice(c * vel, (c + 1) * vel)
                own = pl.ds(pl.multiple_of(p * 2 * k, 2 * k), 2 * k)
                after = pl.ds(pl.multiple_of(p * k, k), k)
                left = [high_lhs[d, own, cols], next_high[d, after, cols], rest_lhs[d, own, cols], next_rest[d, after, cols]]
                main = dot(jnp.concatenate(left, axis=0), high)
                total += main[: 3 * k] + main[3 * k :] + dot(jnp.concatenate(left[:2], axis=0), rest)
            even, odd, after = total[:k], total[k : 2 * k], total[2 * k :]
            if d == 0:
                here += jnp.where(first, even, odd + exchanged(odd))
                moved = jnp.where(first, exchanged(after), 0.0)
                out[:, pl.ds(pl.multiple_of(ahead * width, width), width)] += moved
            else:
                here += jnp.where(first, even + exchanged(even), odd)
                moved = jnp.where(first, 0.0, exchanged(after))
                out[:, pl.ds(pl.multiple_of(behind * width, width), width)] += moved
        out[:, at] += here

    @pl.loop(0, pairs // 2)
    def _(i):
        for u in range(2):
            pair(2 * i + u)


def correct_kernel(plane, part, last, moments, high_lhs, rest_lhs, *refs):
    count = lax.axis_size("gx")
    refs_c, refs = refs[: count - 1], refs[count:]
    entering, outs, (natural, work) = refs[0], refs[1:-2], refs[-2:]
    me = lax.axis_index("gx")
    core = lax.axis_index("vert") % 2
    tiles, whole = 2 * plane // LANES, plane // LANES
    vel = entering.shape[1]
    k = moments.shape[0]
    pairs = moments.shape[1] // (2 * plane)
    rows = min(ROWS, vel)
    low = low_half(rows)
    tail = whole * vel + vel // 2
    passed = [r[tail : tail + 8, :] for r in refs_c]
    scale = []
    for s in range(1, count):
        q = me ^ s
        product = jnp.ones((8, LANES), f32)
        for z in range(1, count):
            if z != s:
                h = me ^ z
                between = ((q < h) & (h < me)) | ((me < h) & (h < q))
                product = product * jnp.where(between, passed[z - 1], 1.0)
        product = product * passed[s - 1]
        scale.append((jnp.where(q < me, product, 0.0), jnp.where(q > me, product, 0.0)))
    for sub in range(vel // rows):
        row = sub * rows
        full = [[jnp.zeros((rows, LANES), f32)] * whole for _ in range(2)]
        half = [jnp.zeros((rows, LANES), f32) for _ in range(2)]
        for s in range(1, count):
            ref = refs_c[s - 1]
            packed = ref[whole * vel + row // 2 : whole * vel + (row + rows) // 2, :]
            ends = jnp.concatenate([packed, turn(packed)], axis=0)
            for d in range(2):
                by = jnp.concatenate(
                    [
                        jnp.broadcast_to(scale[s - 1][d][:, j : j + 1], (8, LANES))
                        for j in range(row // 8, (row + rows) // 8)
                    ],
                    axis=0,
                )
                full[d] = [full[d][w] + by * ref[w * vel + row : w * vel + row + rows, :] for w in range(whole)]
                half[d] = half[d] + by * ends
        for d in range(2):
            cell = full[d] + [half[d]]
            for t in range(whole + 1):
                natural[d, row : row + rows, t * LANES : (t + 1) * LANES] = cell[t]
            turned = [turn(x) for x in cell]
            pair = full[d] + [jnp.where(low, half[d], turned[0])]
            for w in range(whole):
                pair.append(jnp.where(low, turned[w], turned[w + 1]))
            for t in range(tiles):
                entering[d, row : row + rows, t * LANES : (t + 1) * LANES] = pair[t]
    low = low_half(k)
    cols = slice(part * vel, (part + 1) * vel)
    for d in range(2):
        high, rest = halves(natural[d])
        total = dot(high_lhs[d, :, cols], high) + dot(rest_lhs[d, :, cols], high) + dot(high_lhs[d, :, cols], rest)
        if d == 0:
            work[...] = total
        else:
            work[...] += total
    half_pairs = pairs // 2
    width = 2 * plane

    def corrected(p):
        first, second = (
            [work[(2 * p + i) * k : (2 * p + i + 1) * k, t : t + LANES] for t in range(0, (whole + 1) * LANES, LANES)]
            for i in range(2)
        )
        turned = [turn(x) for x in second]
        term = first[:whole] + [jnp.where(low, first[whole], turned[0])]
        term += [jnp.where(low, turned[w], turned[w + 1]) for w in range(whole)]
        return moments[:, p * width : (p + 1) * width] + jnp.concatenate(term, axis=1)

    if not last:
        for p in range(pairs):
            outs[0][:, p * width : (p + 1) * width] = corrected(p)
        return
    for n in range(2):

        @pl.when(core == n)
        def _():
            for p in range(pairs):
                out = outs[(p // half_pairs) ^ n]
                out[:, p % half_pairs * width : (p % half_pairs + 1) * width] = corrected(p)


def fit_rows(m):
    density = 1.0 + 0.5 * jnp.tanh(m[0])
    u = [0.5 * jnp.tanh(m[j]) for j in (1, 2, 3)]
    inverse = 1.0 / (1.0 + 0.5 * jnp.tanh(m[4]))
    s = [0.2 * jnp.tanh(m[j]) for j in range(5, 10)]
    q = [0.2 * jnp.tanh(m[j]) for j in range(10, 13)]
    h = 0.5 * inverse
    uu = u[0] * u[0] + u[1] * u[1] + u[2] * u[2]
    qu = q[0] * u[0] + q[1] * u[1] + q[2] * u[2]
    e = h * 1.4426950408889634
    exponent = [-e * uu, 2.0 * e * u[0], 2.0 * e * u[1], 2.0 * e * u[2], -e, -e, -e]
    a = h * uu - 2.5
    xx, yy, zz = 0.5 * s[3], 0.5 * s[4], -0.5 * (s[3] + s[4])
    xy, xz, yz = s[0], s[1], s[2]
    gx = xx * u[0] + 0.5 * (xy * u[1] + xz * u[2])
    gy = yy * u[1] + 0.5 * (xy * u[0] + yz * u[2])
    gz = zz * u[2] + 0.5 * (xz * u[0] + yz * u[1])
    form = gx * u[0] + gy * u[1] + gz * u[2]
    two = 2.0 * h
    scale = density * inverse * jnp.sqrt(inverse)
    by = scale * inverse
    square = qu * h
    terms = [
        scale + by * (form - qu * a),
        by * (a * q[0] + two * qu * u[0] - 2.0 * gx),
        by * (a * q[1] + two * qu * u[1] - 2.0 * gy),
        by * (a * q[2] + two * qu * u[2] - 2.0 * gz),
        by * (xx - two * q[0] * u[0] - square),
        by * (yy - two * q[1] * u[1] - square),
        by * (zz - two * q[2] * u[2] - square),
        by * (xy - two * (q[0] * u[1] + q[1] * u[0])),
        by * (xz - two * (q[0] * u[2] + q[2] * u[0])),
        by * (yz - two * (q[1] * u[2] + q[2] * u[1])),
        by * (h * q[0]),
        by * (h * q[1]),
        by * (h * q[2]),
    ]
    return exponent, terms


def stacked_right(x):
    a, b, c = thirds(x)
    return jnp.concatenate([a, b, a, c, b, a, jnp.zeros((LANES - 96, x.shape[1]), bf16)], axis=0)


def table_kernel(velocity, relax, reach, _, left_e, left_p, left_r):
    for d in range(2):
        fraction = relax[d]
        x, y, z = (velocity[j, d] for j in range(3))
        xx, yy, zz = x * x, y * y, z * z
        square = xx + yy + zz
        rows = [jnp.ones_like(x), x, y, z, xx, yy, zz, x * y, x * z, y * z, x * square, y * square, z * square]
        rows = jnp.concatenate(rows + [jnp.zeros_like(x)] * (16 - len(rows)), axis=0)
        for ref, value in ((left_e, rows), (left_p, rows * fraction)):
            a, b, c = (t.astype(f32) for t in thirds(value))
            stack = [a, a, b, a, b, c]
            rest = ref.shape[2] - 16 * len(stack)
            if rest:
                stack.append(jnp.zeros((rest, value.shape[1]), f32))
            ref[d, :, :] = jnp.concatenate(stack, axis=0).T.astype(bf16)
        left_r[d, :, :] = turned_thirds(reach[d] * (1.0 - fraction), left_r.shape[2])


def fit_kernel(plane, own, rest, macro, right_e, right_p, tiles, turned, fitted):
    me, count = lax.axis_index("gx"), lax.axis_size("gx")
    core = lax.axis_index("vert") % 2
    lanes = macro.shape[1]
    margin = SMOOTH * plane // LANES
    inner = lanes // LANES
    half = inner // 2
    k = own.shape[0]
    number = inner + 2 * margin
    whole = plane // LANES
    low = low_half(k)
    tile = lambda t: slice(t % number * k, t % number * k + k)
    column = lambda t: slice(t * LANES, (t + 1) * LANES)

    for first, left, right in ((0, own, rest), (1, rest, own)):

        @pl.when(core == first)
        def _():
            for t in range(margin):
                tiles[tile(t), :] = left[:, column(half + t)]
                tiles[tile(margin + inner + t), :] = right[:, column(half + t)]
            for t in range(half):
                tiles[tile(margin + t), :] = left[:, column(t)]
                tiles[tile(margin + half + t), :] = right[:, column(t)]

    before = jnp.where(me > 0, RATE, 0.0)
    after = jnp.where(me < count - 1, RATE, 0.0)
    for _ in range(SMOOTH):
        for t in range(number):
            turned[tile(t), :] = turn(tiles[tile(t), :])
        for t in range(number):
            value = tiles[tile(t), :]
            behind = jnp.where(low, turned[tile(t - whole - 1), :], turned[tile(t - whole), :])
            ahead = jnp.where(low, turned[tile(t + whole), :], turned[tile(t + whole + 1), :])
            rate = (before if t < margin else after if t >= margin + inner else RATE) / (1.0 + value[0:1] * value[0:1])
            tiles[tile(t), :] = value + rate * (behind + ahead - 2.0 * value)

    fitted[...] = jnp.zeros(fitted.shape, f32)
    some = 8
    for t in range(0, inner, some):
        values = [tiles[pl.ds((margin + t) * k + j, some, stride=k), :] for j in range(macro.shape[0])]
        for n, group in enumerate(fit_rows(values)):
            for j, value in enumerate(group):
                fitted[pl.ds((n * inner + t) * k + j, some, stride=k), :] = value
    for t in range(inner):
        macro[:, column(t)] = tiles[tile(margin + t), :][: macro.shape[0]]
        for n, right in enumerate((right_e, right_p)):
            right[:, column(t)] = stacked_right(fitted[(n * inner + t) * k : (n * inner + t + 1) * k, :])


def join_kernel(plane, d, offset, sums, entering, left, spread, _, kept):
    vel = sums.shape[1]
    width = 2 * plane
    tiles, whole = width // LANES, plane // LANES
    pairs = sums.shape[2] // width
    rows = min(ROWS, vel)
    low = low_half(rows)

    def pair(i):
        p = i if d == 1 else pairs - 1 - i
        before = jnp.minimum(p + 1, pairs - 1) if d == 1 else jnp.maximum(p - 1, 0)
        there = jnp.where(i == pairs - 1, 0.0, 1.0)
        place = lambda q, t: pl.ds(pl.multiple_of(q * width + t * LANES, LANES), LANES)
        crossed = []
        for row in range(0, vel, rows):
            line = slice(row, row + rows)
            own = [sums[d, line, place(p, t)] for t in range(tiles)]
            past = [
                None if (t < whole) != (d == 1) and t != whole else there * sums[d, line, place(before, t)]
                for t in range(tiles)
            ]
            crossed.append(swap_cells(seen_before(own, past, d == 1, whole, low), whole, low))
        right = spread[:, pl.ds(pl.multiple_of(p * width, width), width)]
        reach = dot(left[d, offset : offset + vel, :], right)
        for n, row in enumerate(range(0, vel, rows)):
            line = slice(row, row + rows)
            for t in range(tiles):
                tile = slice(t * LANES, (t + 1) * LANES)
                value = sums[d, line, place(p, t)] + crossed[n][t] + entering[d, line, tile]
                kept[d, line, place(p, t)] = reach[line, tile] * value

    @pl.loop(0, pairs // GROUP)
    def _(i):
        for u in range(GROUP):
            pair(i * GROUP + u)


def edge_of(x, width):
    return jnp.where(lax.axis_index("vert") % 2 == 0, x[:, :width], x[:, x.shape[1] - width :])


def add_kernel(a, b, *refs):
    out = refs[-1]
    out[...] = a[...] + b[...]


def edge_kernel(a, b, *refs):
    out, edge = refs[-2:]
    out[...] = a[...] + b[...]
    edge[...] = edge_of(out, edge.shape[1])


def close_kernel(a, b, halo, more, *refs):
    out, lanes = refs[-1], a.shape[1]
    out[:, :lanes] = a[...] + b[...]
    out[:, lanes:] = halo[...] + more[...]


def finish_kernel(plane, parts, *refs):
    kept = refs[:parts]
    left_e, left_p, right_e, right_p, updated = refs[parts:]
    vel = kept[0].shape[1]
    width = 4 * plane
    block = min(vel, 2 * BLOCK)

    def body(*outs):
        at = pl.ds(pl.multiple_of(pl.program_id(0) * width, width), width)
        be, bp = right_e[:, at], right_p[:, at]
        for d in range(2):
            for c in range(parts):
                for row in range(0, vel, block):
                    there = slice(c * vel + row, c * vel + row + block)
                    equil = jnp.exp2(dot(left_e[d, there, :], be)) * dot(left_p[d, there, :], bp)
                    outs[d][there, :] = kept[c][d, row : row + block, at] + equil

    spec = lambda d: pl.BlockSpec((None, updated.shape[1], width), lambda i: (d, 0, i))
    pltpu.emit_pipeline(body, grid=(updated.shape[2] // width,), out_specs=[spec(0), spec(1)])(updated, updated)


def in_vmem(x):
    return pltpu.with_memory_space_constraint(x, pltpu.VMEM)


def per_device(dist, factors, velocity, weights, relax):
    _, vel, lanes = dist.shape
    cells = factors.shape[2]
    plane = lanes // cells
    count = lax.axis_size("gx")
    moments_n = weights.shape[0]
    k = 16
    pairs = cells // 2
    tiles, whole = 2 * plane // LANES, plane // LANES
    width = 2 * plane
    vel_part = vel // PARTS
    vmem = pl.BlockSpec(memory_space=pltpu.VMEM)
    anywhere = pl.BlockSpec(memory_space=pl.ANY)
    params = pltpu.CompilerParams(vmem_limit_bytes=12 * MIB)

    depth = -(-3 * cells // LANES) * LANES
    rows = min(BLOCK, vel_part)
    payload = whole * vel_part + vel_part // 2 + 8
    hbm = pl.BlockSpec(memory_space=pltpu.HBM)
    dist = pltpu.with_memory_space_constraint(dist, pltpu.HBM)
    table = pltpu.with_memory_space_constraint(jnp.swapaxes(factors, 1, 2), pltpu.HBM)
    shared = [
        jax.ShapeDtypeStruct((2, cells, vel), f32),
        pltpu.VMEM((2, vel, depth), bf16),
        pltpu.VMEM((2 * PARTS, 8, LANES), f32),
        pltpu.VMEM((depth, lanes), bf16),
    ]
    swept, sent = [], []
    for part in range(PARTS):
        out, *leaving = pl.pallas_call(
            lambda *refs, part=part: sweep_kernel(part, rows, plane, PARTS, count, *refs),
            out_shape=[pltpu.VMEM((2, vel_part, lanes), f32)]
            + [jax.ShapeDtypeStruct((payload, LANES), f32)] * (count - 1)
            + ([] if part else shared),
            in_specs=[hbm] + ([vmem] * 3 if part else [hbm]),
            out_specs=[vmem] * (count + (0 if part else len(shared))),
            scratch_shapes=[pltpu.VMEM((3, rows, lanes), f32), pltpu.SemaphoreType.DMA((3,))]
            + ([] if part else [pltpu.VMEM((2, cells, vel), f32), pltpu.SemaphoreType.DMA(())]),
            compiler_params=params,
            name="sweep",
        )(dist, *([gain, ends, spread] if part else [table]))
        if part == 0:
            leaving, (reach, gain, ends, spread) = leaving[: count - 1], leaving[count - 1 :]
            gain, ends, spread = in_vmem(gain), in_vmem(ends), in_vmem(spread)
        swept.append(in_vmem(out))
        sent.append(leaving)

    padded = jnp.pad(jnp.moveaxis(weights, 1, 0), ((0, 0), (0, k - moments_n), (0, 0)))
    moments, *lhs = pl.pallas_call(
        lambda *refs: moment_kernel(plane, PARTS, *refs),
        out_shape=[jax.ShapeDtypeStruct((k, lanes), f32)]
        + [pltpu.VMEM((2, 2 * pairs * k, vel), bf16)] * 2,
        in_specs=[vmem] * (2 + PARTS),
        out_specs=[vmem] * 3,
        scratch_shapes=[pltpu.VMEM((2, pairs * k, vel), bf16)] * 2,
        compiler_params=params,
        name="moments",
    )(reach, padded, *swept)

    left_e, left_p, left_r = pl.pallas_call(
        table_kernel,
        out_shape=[pltpu.VMEM((2, vel, LANES), bf16)] * 2 + [pltpu.VMEM((2, vel, depth), bf16)],
        in_specs=[vmem] * 3 + [anywhere],
        out_specs=[vmem] * 3,
        compiler_params=params,
        name="tables",
    )(velocity[:, :, None, :], relax[:, None, :], reach, moments)

    entering = []
    for part in range(PARTS):
        last = part == PARTS - 1
        got = [
            lax.ppermute(sent[part][s - 1], "gx", [(i, i ^ s) for i in range(count)]) for s in range(1, count)
        ]
        out = [jax.ShapeDtypeStruct((k, lanes // 2), f32)] * 2 if last else [jax.ShapeDtypeStruct((k, lanes), f32)]
        found, *moments = pl.pallas_call(
            lambda *refs, part=part, last=last: correct_kernel(plane, part, last, *refs),
            out_shape=[pltpu.VMEM((2, vel_part, width), f32)] + out,
            in_specs=[vmem] * (3 + len(got)) + [anywhere],
            out_specs=[vmem] * (1 + len(out)),
            scratch_shapes=[
                pltpu.VMEM((2, vel_part, (whole + 1) * LANES), f32),
                pltpu.VMEM((2 * pairs * k, (whole + 1) * LANES), f32),
            ],
            compiler_params=params,
            name="correct",
        )(*(moments if part else [moments]), *[in_vmem(x) for x in lhs], *got, left_r)
        entering.append(in_vmem(found))
    mine, other = moments

    size = lax.axis_size("vert")
    margin = SMOOTH * plane
    half = (k, lanes // 2)
    kept = list(swept)

    def join(part, d, after):
        kept[part] = pl.pallas_call(
            lambda *refs: join_kernel(plane, d, part * vel_part, *refs),
            out_shape=pltpu.VMEM(kept[part].shape, f32),
            in_specs=[vmem] * 4 + [anywhere],
            out_specs=vmem,
            input_output_aliases={0: 0},
            compiler_params=params,
            cost_estimate=pl.CostEstimate(
                flops=4 * dist.size * LANES // (2 * PARTS), bytes_accessed=4 * dist.size // PARTS, transcendentals=0
            ),
            name="join",
        )(in_vmem(kept[part]), entering[part], in_vmem(left_r), spread, after)
        return in_vmem(kept[part])

    def combine(kernel, out, *args):
        done = [x for x in args if x is not None]
        return pl.pallas_call(
            kernel,
            out_shape=[jax.ShapeDtypeStruct(x, f32) for x in out],
            in_specs=[vmem] * len(done),
            out_specs=[vmem] * len(out),
            compiler_params=params,
            name=kernel.__name__,
        )(*done)

    steps = [1]
    while 2 * steps[-1] < size:
        steps.append(2 * steps[-1])
    total, beside = mine, None
    chunks = [(part, d) for part in range(PARTS) for d in range(2)]
    for i, step in enumerate(steps[:-1]):
        got = lax.ppermute(total if i else other, "vert", [(v, v ^ step) for v in range(size)])
        if i:
            beside = join(*chunks.pop(0), total) if len(chunks) > 3 else None
        if i == len(steps) - 2:
            total, edge = combine(edge_kernel, [half, (k, margin)], total, got, beside)
        else:
            (total,) = combine(add_kernel, [half], total, got, beside)
    step = steps[-1]
    got = lax.ppermute(total, "vert", [(v, v ^ step) for v in range(size)])
    beyond = []
    for g in range(count - 1):
        for v in range(1, size, 2):
            near, far = g * size + v, (g + 1) * size + v - 1
            beyond += [(near, far), (far, near)]
    halo = lax.ppermute(edge, ("gx", "vert"), beyond)
    join(*chunks.pop(0), total)
    more = lax.ppermute(halo, "vert", [(v, v ^ step) for v in range(size)])
    while len(chunks) > 1:
        join(*chunks.pop(0), halo)
    (own,) = combine(close_kernel, [(k, lanes // 2 + margin)], total, got, halo, more, *[in_vmem(x) for x in kept])
    rest = lax.ppermute(own, "vert", [(v, v ^ 1) for v in range(size)])
    join(*chunks.pop(0), own)

    macro, right_e, right_p = pl.pallas_call(
        lambda *refs: fit_kernel(plane, *refs),
        out_shape=[jax.ShapeDtypeStruct((moments_n, lanes), f32)] + [pltpu.VMEM((LANES, lanes), bf16)] * 2,
        in_specs=[vmem] * 2,
        out_specs=[vmem] * 3,
        scratch_shapes=[pltpu.VMEM(((lanes + 2 * margin) // LANES * k, LANES), f32)] * 2
        + [pltpu.VMEM((2 * lanes // LANES * k, LANES), f32)],
        compiler_params=params,
        name="fit",
    )(own, rest)

    last = [*kept, left_e, left_p, right_e, right_p]
    updated = pl.pallas_call(
        lambda *refs: finish_kernel(plane, PARTS, *refs),
        out_shape=jax.ShapeDtypeStruct(dist.shape, f32),
        in_specs=[vmem] * len(last),
        out_specs=anywhere,
        compiler_params=params,
        name="finish",
    )(*[in_vmem(x) for x in last])
    return updated, macro


def solution(mesh):
    return jax.shard_map(
        per_device,
        mesh=mesh,
        in_specs=(
            P(None, "vert", "gx"),
            P(None, "vert", "gx"),
            P(None, None, "vert"),
            P(None, None, "vert"),
            P(None, "vert"),
        ),
        out_specs=(P(None, "vert", "gx"), P(None, "gx")),
        check_vma=False,
    )
```

```python
import jax
import jax.numpy as jnp
from jax import lax
from jax.experimental import pallas as pl
from jax.experimental.pallas import tpu as pltpu
from jax.sharding import PartitionSpec as P

SMOOTH = 4
RATE = 0.24
LANES = 128
PARTS = 2
BLOCK = 128
SUB = 32
ROWS = 64
GROUP = 4
MIB = 2**20

f32 = jnp.float32
bf16 = jnp.bfloat16


def dot(a, b):
    return jnp.dot(a, b, preferred_element_type=f32)


def halves(x):
    high = x.astype(bf16)
    return high, (x - high.astype(f32)).astype(bf16)


def thirds(x):
    high = x.astype(bf16)
    rest = x - high.astype(f32)
    middle = rest.astype(bf16)
    return high, middle, (rest - middle.astype(f32)).astype(bf16)


def low_half(rows):
    return lax.broadcasted_iota(jnp.int32, (rows, LANES), 1) < LANES // 2


def turn(x):
    return pltpu.roll(x, LANES // 2, 1)


def swap_cells(pair, whole, low):
    tiles = len(pair)
    return [turn(jnp.where(low, pair[(t + whole + 1) % tiles], pair[(t + whole) % tiles])) for t in range(tiles)]


def other_cell(new, old, backward, whole, low):
    tiles = len(new)
    first, second = (old, new) if backward else (new, old)
    upper = first[:whole] + second[whole:]
    lower = first[: whole + 1] + second[whole + 1 :]
    return [turn(jnp.where(low, lower[(t + whole + 1) % tiles], upper[(t + whole) % tiles])) for t in range(tiles)]


def eights(rows):
    return -(-rows // 8) * 8


def packed_rows(t, tiles, moments):
    rest = moments - 8
    return slice(8 * t, 8 * t + 8), slice(8 * tiles + rest * t, 8 * tiles + rest * (t + 1))


def sweep_rows(rows, load, store, gains, backward, pairs, plane):
    tiles, whole = 2 * plane // LANES, plane // LANES
    low = low_half(rows)
    sums = [jnp.zeros((rows, LANES), f32)] * tiles
    for step in range(pairs):
        p = pairs - 1 - step if backward else step
        gain = gains(p)
        old = sums
        sums = [old[t] + gain[:, t * LANES : (t + 1) * LANES] * load(p, t) for t in range(tiles)]
        for t in range(tiles):
            store(p, t, sums[t])
    crossed = other_cell(sums, old, backward, whole, low)
    return [sums[t] + crossed[t] for t in range(tiles)]


def packed_last(values, backward, whole, low):
    tiles = len(values)
    if backward:
        return values[:whole], values[whole]
    turned = [turn(v) for v in values[whole:]]
    full = [jnp.where(low, turned[i], turned[i + 1]) for i in range(whole)]
    return full, turned[whole]


def prepare(plane, parts, factors, reach, gain, ends, spread):
    cells, vel = factors.shape[1], factors.shape[2]
    depth = spread.shape[0]
    lane = lax.broadcasted_iota(jnp.int32, (8, LANES), 1)
    for d in range(2):
        value = factors[d]
        rows = [value[i : i + 1] for i in range(cells)]
        order = range(cells - 1, -1, -1) if d == 1 else range(cells)
        product = None
        for i in order:
            product = rows[i] if product is None else product * rows[i]
            reach[d, i : i + 1, :] = product
        whole = reach[d]
        gain[d, :, :] = turned_thirds(jnp.sqrt(1.0 - value * value) / whole, depth)
        column = jnp.concatenate([whole[i : i + 1] for i in order][-1:] * 8, axis=0)
        column = column.T
        for c in range(parts):
            tile = jnp.zeros((8, LANES), f32)
            for j in range(vel // parts // 8):
                at = c * (vel // parts) + 8 * j
                tile = jnp.where(lane == j, jnp.broadcast_to(column[at : at + 8, 0:1], (8, LANES)), tile)
            ends[2 * c + d, :, :] = tile
    row = lax.broadcasted_iota(jnp.int32, (cells, LANES), 0)
    low = low_half(cells)
    number = 2 * plane // LANES
    for t in range(spread.shape[1] // LANES):
        cell = t // number * 2
        middle = plane // LANES
        at = t % number
        one = cell if at < middle else cell + 1 if at > middle else jnp.where(low, cell, cell + 1)
        own = jnp.where(row == one, 1.0, 0.0).astype(bf16)
        column = slice(t * LANES, (t + 1) * LANES)
        for i in range(3):
            spread[i * cells : (i + 1) * cells, column] = own
        if depth > 3 * cells:
            spread[3 * cells :, column] = jnp.zeros((depth - 3 * cells, LANES), bf16)


def turned_thirds(x, depth):
    terms = [t.astype(f32) for t in thirds(x)]
    rest = depth - 3 * x.shape[0]
    if rest:
        terms.append(jnp.zeros((rest, x.shape[1]), f32))
    return jnp.concatenate(terms, axis=0).T.astype(bf16)


def sweep_kernel(part, rows, plane, parts, count, *refs):
    if part == 0:
        dist, factors, swept, *sent = refs[: 2 + count]
        reach, gain, ends, spread, blocks, arrived, table, read = refs[2 + count :]
    else:
        dist, gain, ends, spread, swept, *sent = refs[: 4 + count]
        blocks, arrived = refs[4 + count :]
    me = lax.axis_index("gx")
    vel = swept.shape[1]
    pairs = swept.shape[2] // plane // 2
    whole = plane // LANES
    width = 2 * plane
    low = low_half(rows)
    some = min(ROWS, rows)
    steps = [(d, row) for row in range(0, vel, rows) for d in range(2)]
    slots = blocks.shape[0]

    def fetch(i):
        d, row = steps[i]
        at = part * vel + row
        return pltpu.make_async_copy(dist.at[d, at : at + rows, :], blocks.at[i % slots], arrived.at[i % slots])

    if part == 0:
        first = pltpu.make_async_copy(factors, table, read)
        first.start()
    for i in range(min(slots, len(steps))):
        fetch(i).start()
    if part == 0:
        first.wait()
        prepare(plane, parts, table, reach, gain, ends, spread)

    for i, (d, row) in enumerate(steps):
        fetch(i).wait()
        ref = blocks.at[i % slots]
        left = gain[d, part * vel + row : part * vel + row + rows, :]

        def gains(p):
            return dot(left, spread[:, p * width : (p + 1) * width])

        def load(p, t):
            return ref[:, p * width + t * LANES : p * width + (t + 1) * LANES]

        def store(p, t, value):
            swept[d, row : row + rows, p * width + t * LANES : p * width + (t + 1) * LANES] = value

        values = sweep_rows(rows, load, store, gains, d == 1, pairs, plane)
        if i + slots < len(steps):
            fetch(i + slots).start()
        full, half = packed_last(values, d == 1, whole, low)
        both = [
            jnp.where(low[: some // 2], half[n : n + some // 2], turn(half[n + some // 2 : n + some]))
            for n in range(0, rows, some)
        ]
        for s in range(1, count):
            out = sent[s - 1]

            @pl.when(((me ^ s) > me) == (d == 0))
            def _():
                for w in range(whole):
                    out[w * vel + row : w * vel + row + rows, :] = full[w]
                for n, packed in enumerate(both):
                    at = whole * vel + (row + n * some) // 2
                    out[at : at + some // 2, :] = packed

    tail = whole * vel + vel // 2
    for s in range(1, count):
        sent[s - 1][tail : tail + 8, :] = jnp.where((me ^ s) > me, ends[2 * part], ends[2 * part + 1])


def moment_kernel(plane, parts, reach, weight, *refs):
    sums = refs[:parts]
    out, high_lhs, rest_lhs, next_high, next_rest = refs[parts:]
    vel = sums[0].shape[1]
    k = weight.shape[1]
    width = 2 * plane
    pairs = next_high.shape[1] // k
    whole = plane // LANES
    low = low_half(k)
    for d in range(2):
        for p in range(pairs):
            rows = [weight[d] * reach[d, 2 * p : 2 * p + 1, :], weight[d] * reach[d, 2 * p + 1 : 2 * p + 2, :]]
            both = slice(2 * p * k, 2 * (p + 1) * k)
            high_lhs[d, both, :], rest_lhs[d, both, :] = halves(jnp.concatenate(rows, axis=0))
            q = p + 1 if d == 1 else p - 1
            if 0 <= q < pairs:
                at = slice(q * k, (q + 1) * k)
                next_high[d, at, :], next_rest[d, at, :] = halves(rows[d])
        q = 0 if d == 1 else pairs - 1
        at = slice(q * k, (q + 1) * k)
        next_high[d, at, :] = jnp.zeros((k, weight.shape[2]), bf16)
        next_rest[d, at, :] = jnp.zeros((k, weight.shape[2]), bf16)
    first = lax.broadcasted_iota(jnp.int32, (k, width), 1) < plane
    out[...] = jnp.zeros(out.shape, f32)

    def exchanged(x):
        tiles = [x[:, t : t + LANES] for t in range(0, width, LANES)]
        return jnp.concatenate(swap_cells(tiles, whole, low), axis=1)

    def pair(p):
        at = pl.ds(pl.multiple_of(p * width, width), width)
        ahead = jnp.minimum(p + 1, pairs - 1)
        behind = jnp.maximum(p - 1, 0)
        here = jnp.zeros((k, width), f32)
        for d in range(2):
            total = jnp.zeros((3 * k, width), f32)
            for c, part in enumerate(sums):
                high, rest = halves(part[d, :, at])
                cols = slice(c * vel, (c + 1) * vel)
                own = pl.ds(pl.multiple_of(p * 2 * k, 2 * k), 2 * k)
                after = pl.ds(pl.multiple_of(p * k, k), k)
                left = [high_lhs[d, own, cols], next_high[d, after, cols], rest_lhs[d, own, cols], next_rest[d, after, cols]]
                main = dot(jnp.concatenate(left, axis=0), high)
                total += main[: 3 * k] + main[3 * k :] + dot(jnp.concatenate(left[:2], axis=0), rest)
            even, odd, after = total[:k], total[k : 2 * k], total[2 * k :]
            if d == 0:
                here += jnp.where(first, even, odd + exchanged(odd))
                moved = jnp.where(first, exchanged(after), 0.0)
                out[:, pl.ds(pl.multiple_of(ahead * width, width), width)] += moved
            else:
                here += jnp.where(first, even + exchanged(even), odd)
                moved = jnp.where(first, 0.0, exchanged(after))
                out[:, pl.ds(pl.multiple_of(behind * width, width), width)] += moved
        out[:, at] += here

    @pl.loop(0, pairs // GROUP)
    def _(i):
        for u in range(GROUP):
            pair(GROUP * i + u)


def correct_kernel(plane, part, last, number, moments, high_lhs, rest_lhs, *refs):
    count = lax.axis_size("gx")
    refs_c, refs = refs[: count - 1], refs[count:]
    entering, outs, (natural, work) = refs[0], refs[1:-2], refs[-2:]
    me = lax.axis_index("gx")
    core = lax.axis_index("vert") % 2
    tiles, whole = 2 * plane // LANES, plane // LANES
    vel = entering.shape[1]
    k = moments.shape[0]
    pairs = moments.shape[1] // (2 * plane)
    rows = min(ROWS, vel)
    low = low_half(rows)
    tail = whole * vel + vel // 2
    passed = [r[tail : tail + 8, :] for r in refs_c]
    scale = []
    for s in range(1, count):
        q = me ^ s
        product = jnp.ones((8, LANES), f32)
        for z in range(1, count):
            if z != s:
                h = me ^ z
                between = ((q < h) & (h < me)) | ((me < h) & (h < q))
                product = product * jnp.where(between, passed[z - 1], 1.0)
        product = product * passed[s - 1]
        scale.append((jnp.where(q < me, product, 0.0), jnp.where(q > me, product, 0.0)))
    for sub in range(vel // rows):
        row = sub * rows
        full = [[jnp.zeros((rows, LANES), f32)] * whole for _ in range(2)]
        half = [jnp.zeros((rows, LANES), f32) for _ in range(2)]
        for s in range(1, count):
            ref = refs_c[s - 1]
            packed = ref[whole * vel + row // 2 : whole * vel + (row + rows) // 2, :]
            ends = jnp.concatenate([packed, turn(packed)], axis=0)
            for d in range(2):
                by = jnp.concatenate(
                    [
                        jnp.broadcast_to(scale[s - 1][d][:, j : j + 1], (8, LANES))
                        for j in range(row // 8, (row + rows) // 8)
                    ],
                    axis=0,
                )
                full[d] = [full[d][w] + by * ref[w * vel + row : w * vel + row + rows, :] for w in range(whole)]
                half[d] = half[d] + by * ends
        for d in range(2):
            cell = full[d] + [half[d]]
            for t in range(whole + 1):
                natural[d, row : row + rows, t * LANES : (t + 1) * LANES] = cell[t]
            turned = [turn(x) for x in cell]
            pair = full[d] + [jnp.where(low, half[d], turned[0])]
            for w in range(whole):
                pair.append(jnp.where(low, turned[w], turned[w + 1]))
            for t in range(tiles):
                entering[d, row : row + rows, t * LANES : (t + 1) * LANES] = pair[t]
    low = low_half(k)
    cols = slice(part * vel, (part + 1) * vel)
    for d in range(2):
        high, rest = halves(natural[d])
        total = dot(high_lhs[d, :, cols], high) + dot(rest_lhs[d, :, cols], high) + dot(high_lhs[d, :, cols], rest)
        if d == 0:
            work[...] = total
        else:
            work[...] += total
    half_pairs = pairs // 2
    width = 2 * plane

    def corrected(p):
        first, second = (
            [work[(2 * p + i) * k : (2 * p + i + 1) * k, t : t + LANES] for t in range(0, (whole + 1) * LANES, LANES)]
            for i in range(2)
        )
        turned = [turn(x) for x in second]
        term = first[:whole] + [jnp.where(low, first[whole], turned[0])]
        term += [jnp.where(low, turned[w], turned[w + 1]) for w in range(whole)]
        return moments[:, p * width : (p + 1) * width] + jnp.concatenate(term, axis=1)

    if not last:
        for p in range(pairs):
            outs[0][:, p * width : (p + 1) * width] = corrected(p)
        return
    half_tiles = half_pairs * width // LANES
    for n in range(2):

        @pl.when(core == n)
        def _():
            for p in range(pairs):
                out = outs[(p // half_pairs) ^ n]
                value = corrected(p)
                for t in range(width // LANES):
                    head, tail = packed_rows(p % half_pairs * (width // LANES) + t, half_tiles, number)
                    out[head, :] = value[:8, t * LANES : (t + 1) * LANES]
                    out[tail, :] = value[8:number, t * LANES : (t + 1) * LANES]


def fit_rows(m):
    density = 1.0 + 0.5 * jnp.tanh(m[0])
    u = [0.5 * jnp.tanh(m[j]) for j in (1, 2, 3)]
    inverse = 1.0 / (1.0 + 0.5 * jnp.tanh(m[4]))
    s = [0.2 * jnp.tanh(m[j]) for j in range(5, 10)]
    q = [0.2 * jnp.tanh(m[j]) for j in range(10, 13)]
    h = 0.5 * inverse
    uu = u[0] * u[0] + u[1] * u[1] + u[2] * u[2]
    qu = q[0] * u[0] + q[1] * u[1] + q[2] * u[2]
    e = h * 1.4426950408889634
    exponent = [-e * uu, 2.0 * e * u[0], 2.0 * e * u[1], 2.0 * e * u[2], -e, -e, -e]
    a = h * uu - 2.5
    xx, yy, zz = 0.5 * s[3], 0.5 * s[4], -0.5 * (s[3] + s[4])
    xy, xz, yz = s[0], s[1], s[2]
    gx = xx * u[0] + 0.5 * (xy * u[1] + xz * u[2])
    gy = yy * u[1] + 0.5 * (xy * u[0] + yz * u[2])
    gz = zz * u[2] + 0.5 * (xz * u[0] + yz * u[1])
    form = gx * u[0] + gy * u[1] + gz * u[2]
    two = 2.0 * h
    scale = density * inverse * jnp.sqrt(inverse)
    by = scale * inverse
    square = qu * h
    terms = [
        scale + by * (form - qu * a),
        by * (a * q[0] + two * qu * u[0] - 2.0 * gx),
        by * (a * q[1] + two * qu * u[1] - 2.0 * gy),
        by * (a * q[2] + two * qu * u[2] - 2.0 * gz),
        by * (xx - two * q[0] * u[0] - square),
        by * (yy - two * q[1] * u[1] - square),
        by * (zz - two * q[2] * u[2] - square),
        by * (xy - two * (q[0] * u[1] + q[1] * u[0])),
        by * (xz - two * (q[0] * u[2] + q[2] * u[0])),
        by * (yz - two * (q[1] * u[2] + q[2] * u[1])),
        by * (h * q[0]),
        by * (h * q[1]),
        by * (h * q[2]),
    ]
    return exponent, terms


def stacked_right(x):
    a, b, c = thirds(x)
    return jnp.concatenate([a, b, a, c, b, a, jnp.zeros((LANES - 96, x.shape[1]), bf16)], axis=0)


def table_kernel(velocity, relax, reach, _, left_e, left_p, left_r):
    for d in range(2):
        fraction = relax[d]
        x, y, z = (velocity[j, d] for j in range(3))
        xx, yy, zz = x * x, y * y, z * z
        square = xx + yy + zz
        rows = [jnp.ones_like(x), x, y, z, xx, yy, zz, x * y, x * z, y * z, x * square, y * square, z * square]
        rows = jnp.concatenate(rows + [jnp.zeros_like(x)] * (16 - len(rows)), axis=0)
        for ref, value in ((left_e, rows), (left_p, rows * fraction)):
            a, b, c = (t.astype(f32) for t in thirds(value))
            stack = [a, a, b, a, b, c]
            rest = ref.shape[2] - 16 * len(stack)
            if rest:
                stack.append(jnp.zeros((rest, value.shape[1]), f32))
            ref[d, :, :] = jnp.concatenate(stack, axis=0).T.astype(bf16)
        left_r[d, :, :] = turned_thirds(reach[d] * (1.0 - fraction), left_r.shape[2])


def fit_kernel(plane, k, own, rest, macro, right_e, right_p, tiles, turned, fitted):
    me, count = lax.axis_index("gx"), lax.axis_size("gx")
    core = lax.axis_index("vert") % 2
    lanes = macro.shape[1]
    margin = SMOOTH * plane // LANES
    inner = lanes // LANES
    half = inner // 2
    number = inner + 2 * margin
    whole = plane // LANES
    low = low_half(k)
    tile = lambda t: slice(t % number * k, t % number * k + k)
    column = lambda t: slice(t * LANES, (t + 1) * LANES)

    count_of = macro.shape[0]
    outside = eights(half * count_of)

    def place(t, ref, offset, of, size):
        at = t * k
        for piece, row in zip(packed_rows(of, size, count_of), (at, at + 8)):
            some = piece.stop - piece.start
            tiles[row : row + some, :] = ref[offset + piece.start : offset + piece.stop, :]

    for first, left, right in ((0, own, rest), (1, rest, own)):

        @pl.when(core == first)
        def _():
            for t in range(margin):
                place(t, left, outside, t, margin)
                place(margin + inner + t, right, outside, t, margin)
            for t in range(half):
                place(margin + t, left, 0, t, half)
                place(margin + half + t, right, 0, t, half)

    before = jnp.where(me > 0, RATE, 0.0)
    after = jnp.where(me < count - 1, RATE, 0.0)
    for _ in range(SMOOTH):
        for t in range(number):
            turned[tile(t), :] = turn(tiles[tile(t), :])
        for t in range(number):
            value = tiles[tile(t), :]
            behind = jnp.where(low, turned[tile(t - whole - 1), :], turned[tile(t - whole), :])
            ahead = jnp.where(low, turned[tile(t + whole), :], turned[tile(t + whole + 1), :])
            rate = (before if t < margin else after if t >= margin + inner else RATE) / (1.0 + value[0:1] * value[0:1])
            tiles[tile(t), :] = value + rate * (behind + ahead - 2.0 * value)

    fitted[...] = jnp.zeros(fitted.shape, f32)
    some = 8
    for t in range(0, inner, some):
        values = [tiles[pl.ds((margin + t) * k + j, some, stride=k), :] for j in range(macro.shape[0])]
        for n, group in enumerate(fit_rows(values)):
            for j, value in enumerate(group):
                fitted[pl.ds((n * inner + t) * k + j, some, stride=k), :] = value
    for t in range(inner):
        macro[:, column(t)] = tiles[tile(margin + t), :][: macro.shape[0]]
        for n, right in enumerate((right_e, right_p)):
            right[:, column(t)] = stacked_right(fitted[(n * inner + t) * k : (n * inner + t + 1) * k, :])


def join_kernel(plane, d, offset, span, sums, entering, left, spread, _, kept):
    vel = sums.shape[1]
    width = 2 * plane
    tiles, whole = width // LANES, plane // LANES
    pairs = sums.shape[2] // width
    rows = min(ROWS, vel)
    low = low_half(rows)

    def pair(i):
        p = i if d == 1 else pairs - 1 - i
        before = jnp.minimum(p + 1, pairs - 1) if d == 1 else jnp.maximum(p - 1, 0)
        there = jnp.where(i == pairs - 1, 0.0, 1.0)
        place = lambda q, t: pl.ds(pl.multiple_of(q * width + t * LANES, LANES), LANES)
        crossed = []
        for row in range(0, vel, rows):
            line = slice(row, row + rows)
            own = [sums[d, line, place(p, t)] for t in range(tiles)]
            past = [
                None if (t < whole) != (d == 1) and t != whole else there * sums[d, line, place(before, t)]
                for t in range(tiles)
            ]
            crossed.append(other_cell(own, past, d == 1, whole, low))
        right = spread[:, pl.ds(pl.multiple_of(p * width, width), width)]
        reach = dot(left[d, offset : offset + vel, :], right)
        for n, row in enumerate(range(0, vel, rows)):
            line = slice(row, row + rows)
            for t in range(tiles):
                tile = slice(t * LANES, (t + 1) * LANES)
                value = sums[d, line, place(p, t)] + crossed[n][t] + entering[d, line, tile]
                kept[d, line, place(p, t)] = reach[line, tile] * value

    @pl.loop(*span)
    def _(i):
        for u in range(GROUP):
            pair(i * GROUP + u)


def add_kernel(a, b, *refs):
    out = refs[-1]
    out[...] = a[...] + b[...]


def edge_kernel(margin, number, a, b, *refs):
    out, edge = refs[-2:]
    out[...] = a[...] + b[...]
    first = lax.axis_index("vert") % 2 == 0
    tiles = out.shape[0] // number
    rest = number - 8
    for start, size, into in ((0, 8, 0), (8 * tiles, rest, 8 * margin)):
        low = out[start : start + size * margin, :]
        high = out[start + size * (tiles - margin) : start + size * tiles, :]
        edge[into : into + size * margin, :] = jnp.where(first, low, high)
    if edge.shape[0] > number * margin:
        edge[number * margin :, :] = jnp.zeros((edge.shape[0] - number * margin, LANES), f32)


def close_kernel(a, b, halo, more, *refs):
    out, rows = refs[-1], a.shape[0]
    out[:rows, :] = a[...] + b[...]
    out[rows:, :] = halo[...] + more[...]


def finish_kernel(plane, parts, *refs):
    kept = refs[:parts]
    left_e, left_p, right_e, right_p, updated = refs[parts:]
    vel = kept[0].shape[1]
    width = 4 * plane
    block = min(vel, 2 * BLOCK)

    def body(*outs):
        at = pl.ds(pl.multiple_of(pl.program_id(0) * width, width), width)
        be, bp = right_e[:, at], right_p[:, at]
        for d in range(2):
            for c in range(parts):
                for row in range(0, vel, block):
                    there = slice(c * vel + row, c * vel + row + block)
                    equil = jnp.exp2(dot(left_e[d, there, :], be)) * dot(left_p[d, there, :], bp)
                    outs[d][there, :] = kept[c][d, row : row + block, at] + equil

    spec = lambda d: pl.BlockSpec((None, updated.shape[1], width), lambda i: (d, 0, i))
    pltpu.emit_pipeline(body, grid=(updated.shape[2] // width,), out_specs=[spec(0), spec(1)])(updated, updated)


def in_vmem(x):
    return pltpu.with_memory_space_constraint(x, pltpu.VMEM)


def per_device(dist, factors, velocity, weights, relax):
    _, vel, lanes = dist.shape
    cells = factors.shape[2]
    plane = lanes // cells
    count = lax.axis_size("gx")
    moments_n = weights.shape[0]
    k = 16
    pairs = cells // 2
    tiles, whole = 2 * plane // LANES, plane // LANES
    width = 2 * plane
    vel_part = vel // PARTS
    vmem = pl.BlockSpec(memory_space=pltpu.VMEM)
    anywhere = pl.BlockSpec(memory_space=pl.ANY)
    params = pltpu.CompilerParams(vmem_limit_bytes=12 * MIB)

    depth = -(-3 * cells // LANES) * LANES
    rows = min(BLOCK, vel_part)
    payload = whole * vel_part + vel_part // 2 + 8
    hbm = pl.BlockSpec(memory_space=pltpu.HBM)
    dist = pltpu.with_memory_space_constraint(dist, pltpu.HBM)
    table = pltpu.with_memory_space_constraint(jnp.swapaxes(factors, 1, 2), pltpu.HBM)
    shared = [
        jax.ShapeDtypeStruct((2, cells, vel), f32),
        pltpu.VMEM((2, vel, depth), bf16),
        pltpu.VMEM((2 * PARTS, 8, LANES), f32),
        pltpu.VMEM((depth, lanes), bf16),
    ]
    swept, sent = [], []
    for part in range(PARTS):
        out, *leaving = pl.pallas_call(
            lambda *refs, part=part: sweep_kernel(part, rows, plane, PARTS, count, *refs),
            out_shape=[pltpu.VMEM((2, vel_part, lanes), f32)]
            + [jax.ShapeDtypeStruct((payload, LANES), f32)] * (count - 1)
            + ([] if part else shared),
            in_specs=[hbm] + ([vmem] * 3 if part else [hbm]),
            out_specs=[vmem] * (count + (0 if part else len(shared))),
            scratch_shapes=[pltpu.VMEM((3, rows, lanes), f32), pltpu.SemaphoreType.DMA((3,))]
            + ([] if part else [pltpu.VMEM((2, cells, vel), f32), pltpu.SemaphoreType.DMA(())]),
            compiler_params=params,
            name="sweep",
        )(dist, *([gain, ends, spread] if part else [table]))
        if part == 0:
            leaving, (reach, gain, ends, spread) = leaving[: count - 1], leaving[count - 1 :]
            gain, ends, spread = in_vmem(gain), in_vmem(ends), in_vmem(spread)
        swept.append(in_vmem(out))
        sent.append(leaving)

    padded = jnp.pad(jnp.moveaxis(weights, 1, 0), ((0, 0), (0, k - moments_n), (0, 0)))
    moments, *lhs = pl.pallas_call(
        lambda *refs: moment_kernel(plane, PARTS, *refs),
        out_shape=[jax.ShapeDtypeStruct((k, lanes), f32)]
        + [pltpu.VMEM((2, 2 * pairs * k, vel), bf16)] * 2,
        in_specs=[vmem] * (2 + PARTS),
        out_specs=[vmem] * 3,
        scratch_shapes=[pltpu.VMEM((2, pairs * k, vel), bf16)] * 2,
        compiler_params=params,
        name="moments",
    )(reach, padded, *swept)

    left_e, left_p, left_r = pl.pallas_call(
        table_kernel,
        out_shape=[pltpu.VMEM((2, vel, LANES), bf16)] * 2 + [pltpu.VMEM((2, vel, depth), bf16)],
        in_specs=[vmem] * 3 + [anywhere],
        out_specs=[vmem] * 3,
        compiler_params=params,
        name="tables",
    )(velocity[:, :, None, :], relax[:, None, :], reach, moments)

    margin = SMOOTH * plane // LANES
    half = (eights(lanes // 2 // LANES * moments_n), LANES)
    side = (eights(margin * moments_n), LANES)
    kept = list(swept)

    def join(part, d, start, stop, after):
        span = tuple(x * (pairs // GROUP) // 4 for x in (start, stop))
        kept[part] = pl.pallas_call(
            lambda *refs: join_kernel(plane, d, part * vel_part, span, *refs),
            out_shape=pltpu.VMEM(kept[part].shape, f32),
            in_specs=[vmem] * 4 + [anywhere],
            out_specs=vmem,
            input_output_aliases={0: 0},
            compiler_params=params,
            cost_estimate=pl.CostEstimate(
                flops=dist.size * LANES * (stop - start) // (2 * PARTS),
                bytes_accessed=dist.size * (stop - start) // PARTS,
                transcendentals=0,
            ),
            name="join",
        )(in_vmem(kept[part]), entering[part], in_vmem(left_r), spread, after)
        return in_vmem(kept[part])

    entering = []
    for part in range(PARTS):
        last = part == PARTS - 1
        got = [
            lax.ppermute(sent[part][s - 1], "gx", [(i, i ^ s) for i in range(count)]) for s in range(1, count)
        ]
        out = [jax.ShapeDtypeStruct(half, f32)] * 2 if last else [jax.ShapeDtypeStruct((k, lanes), f32)]
        found, *moments = pl.pallas_call(
            lambda *refs, part=part, last=last: correct_kernel(plane, part, last, moments_n, *refs),
            out_shape=[pltpu.VMEM((2, vel_part, width), f32)] + out,
            in_specs=[vmem] * (3 + len(got)) + [anywhere],
            out_specs=[vmem] * (1 + len(out)),
            scratch_shapes=[
                pltpu.VMEM((2, vel_part, (whole + 1) * LANES), f32),
                pltpu.VMEM((2 * pairs * k, (whole + 1) * LANES), f32),
            ],
            compiler_params=params,
            name="correct",
        )(*(moments if part else [moments]), *[in_vmem(x) for x in lhs], *got, early if part else left_r)
        entering.append(in_vmem(found))
        if not last:
            early = join(part, 0, 0, 2, found)
    mine, other = moments

    size = lax.axis_size("vert")
    def combine(kernel, out, *args):
        done = [x for x in args if x is not None]
        return pl.pallas_call(
            kernel,
            out_shape=[jax.ShapeDtypeStruct(x, f32) for x in out],
            in_specs=[vmem] * len(done),
            out_specs=[vmem] * len(out),
            compiler_params=params,
            name="add",
        )(*done)

    steps = [1]
    while 2 * steps[-1] < size:
        steps.append(2 * steps[-1])
    total, beside = mine, None
    for i, step in enumerate(steps[:-1]):
        got = lax.ppermute(total if i else other, "vert", [(v, v ^ step) for v in range(size)])
        if i == 1:
            join(0, 0, 2, 4, total)
            beside = join(0, 1, 0, 2, total)
        if i == len(steps) - 2:
            total, edge = combine(
                lambda *refs: edge_kernel(margin, moments_n, *refs), [half, side], total, got, beside
            )
        else:
            (total,) = combine(add_kernel, [half], total, got, beside)
    step = steps[-1]
    got = lax.ppermute(total, "vert", [(v, v ^ step) for v in range(size)])
    beyond = []
    for g in range(count - 1):
        for v in range(1, size, 2):
            near, far = g * size + v, (g + 1) * size + v - 1
            beyond += [(near, far), (far, near)]
    halo = lax.ppermute(edge, ("gx", "vert"), beyond)
    join(1, 0, 0, 4, total)
    more = lax.ppermute(halo, "vert", [(v, v ^ step) for v in range(size)])
    join(0, 1, 2, 4, halo)
    join(1, 1, 0, 2, halo)
    (own,) = combine(close_kernel, [(half[0] + side[0], LANES)], total, got, halo, more, *[in_vmem(x) for x in kept])
    rest = lax.ppermute(own, "vert", [(v, v ^ 1) for v in range(size)])
    join(1, 1, 2, 4, own)

    macro, right_e, right_p = pl.pallas_call(
        lambda *refs: fit_kernel(plane, k, *refs),
        out_shape=[jax.ShapeDtypeStruct((moments_n, lanes), f32)] + [pltpu.VMEM((LANES, lanes), bf16)] * 2,
        in_specs=[vmem] * 2,
        out_specs=[vmem] * 3,
        scratch_shapes=[pltpu.VMEM((((lanes // LANES) + 2 * margin) * k, LANES), f32)] * 2
        + [pltpu.VMEM((2 * lanes // LANES * k, LANES), f32)],
        compiler_params=params,
        name="fit",
    )(own, rest)

    last = [*kept, left_e, left_p, right_e, right_p]
    updated = pl.pallas_call(
        lambda *refs: finish_kernel(plane, PARTS, *refs),
        out_shape=jax.ShapeDtypeStruct(dist.shape, f32),
        in_specs=[vmem] * len(last),
        out_specs=anywhere,
        compiler_params=params,
        name="finish",
    )(*[in_vmem(x) for x in last])
    return updated, macro


def solution(mesh):
    return jax.shard_map(
        per_device,
        mesh=mesh,
        in_specs=(
            P(None, "vert", "gx"),
            P(None, "vert", "gx"),
            P(None, None, "vert"),
            P(None, None, "vert"),
            P(None, "vert"),
        ),
        out_specs=(P(None, "vert", "gx"), P(None, "gx")),
        check_vma=False,
    )
```

```python
import jax
import jax.numpy as jnp
from jax import lax
from jax.experimental import pallas as pl
from jax.experimental.pallas import tpu as pltpu
from jax.sharding import PartitionSpec as P

SMOOTH = 4
RATE = 0.24
LANES = 128
PARTS = 2
BLOCK = 128
SUB = 32
ROWS = 64
GROUP = 4
MIB = 2**20

f32 = jnp.float32
bf16 = jnp.bfloat16


def dot(a, b):
    return jnp.dot(a, b, preferred_element_type=f32)


def halves(x):
    high = x.astype(bf16)
    return high, (x - high.astype(f32)).astype(bf16)


def thirds(x):
    high = x.astype(bf16)
    rest = x - high.astype(f32)
    middle = rest.astype(bf16)
    return high, middle, (rest - middle.astype(f32)).astype(bf16)


def low_half(rows):
    return lax.broadcasted_iota(jnp.int32, (rows, LANES), 1) < LANES // 2


def turn(x):
    return pltpu.roll(x, LANES // 2, 1)


def swap_cells(pair, whole, low):
    tiles = len(pair)
    return [turn(jnp.where(low, pair[(t + whole + 1) % tiles], pair[(t + whole) % tiles])) for t in range(tiles)]


def other_cell(new, old, backward, whole, low):
    tiles = len(new)
    first, second = (old, new) if backward else (new, old)
    upper = first[:whole] + second[whole:]
    lower = first[: whole + 1] + second[whole + 1 :]
    return [turn(jnp.where(low, lower[(t + whole + 1) % tiles], upper[(t + whole) % tiles])) for t in range(tiles)]


def eights(rows):
    return -(-rows // 8) * 8


def packed_rows(t, tiles, moments):
    rest = moments - 8
    return slice(8 * t, 8 * t + 8), slice(8 * tiles + rest * t, 8 * tiles + rest * (t + 1))


def sweep_rows(rows, load, store, gains, backward, pairs, plane):
    tiles, whole = 2 * plane // LANES, plane // LANES
    low = low_half(rows)
    sums = [jnp.zeros((rows, LANES), f32)] * tiles
    for step in range(pairs):
        p = pairs - 1 - step if backward else step
        gain = gains(p)
        old = sums
        sums = [old[t] + gain[:, t * LANES : (t + 1) * LANES] * load(p, t) for t in range(tiles)]
        for t in range(tiles):
            store(p, t, sums[t])
    crossed = other_cell(sums, old, backward, whole, low)
    return [sums[t] + crossed[t] for t in range(tiles)]


def packed_last(values, backward, whole, low):
    tiles = len(values)
    if backward:
        return values[:whole], values[whole]
    turned = [turn(v) for v in values[whole:]]
    full = [jnp.where(low, turned[i], turned[i + 1]) for i in range(whole)]
    return full, turned[whole]


def prepare(plane, parts, factors, reach, gain, ends, spread):
    cells, vel = factors.shape[1], factors.shape[2]
    depth = spread.shape[0]
    lane = lax.broadcasted_iota(jnp.int32, (8, LANES), 1)
    for d in range(2):
        value = factors[d]
        rows = [value[i : i + 1] for i in range(cells)]
        order = range(cells - 1, -1, -1) if d == 1 else range(cells)
        product = None
        for i in order:
            product = rows[i] if product is None else product * rows[i]
            reach[d, i : i + 1, :] = product
        whole = reach[d]
        gain[d, :, :] = turned_thirds(jnp.sqrt(1.0 - value * value) / whole, depth)
        column = jnp.concatenate([whole[i : i + 1] for i in order][-1:] * 8, axis=0)
        column = column.T
        for c in range(parts):
            tile = jnp.zeros((8, LANES), f32)
            for j in range(vel // parts // 8):
                at = c * (vel // parts) + 8 * j
                tile = jnp.where(lane == j, jnp.broadcast_to(column[at : at + 8, 0:1], (8, LANES)), tile)
            ends[2 * c + d, :, :] = tile
    row = lax.broadcasted_iota(jnp.int32, (cells, LANES), 0)
    low = low_half(cells)
    number = 2 * plane // LANES
    for t in range(spread.shape[1] // LANES):
        cell = t // number * 2
        middle = plane // LANES
        at = t % number
        one = cell if at < middle else cell + 1 if at > middle else jnp.where(low, cell, cell + 1)
        own = jnp.where(row == one, 1.0, 0.0).astype(bf16)
        column = slice(t * LANES, (t + 1) * LANES)
        for i in range(3):
            spread[i * cells : (i + 1) * cells, column] = own
        if depth > 3 * cells:
            spread[3 * cells :, column] = jnp.zeros((depth - 3 * cells, LANES), bf16)


def turned_thirds(x, depth):
    terms = [t.astype(f32) for t in thirds(x)]
    rest = depth - 3 * x.shape[0]
    if rest:
        terms.append(jnp.zeros((rest, x.shape[1]), f32))
    return jnp.concatenate(terms, axis=0).T.astype(bf16)


def sweep_kernel(part, rows, plane, parts, count, *refs):
    if part == 0:
        dist, factors, swept, *sent = refs[: 2 + count]
        reach, gain, ends, spread, blocks, arrived, table, read = refs[2 + count :]
    else:
        dist, gain, ends, spread, swept, *sent = refs[: 4 + count]
        blocks, arrived = refs[4 + count :]
    me = lax.axis_index("gx")
    vel = swept.shape[1]
    pairs = swept.shape[2] // plane // 2
    whole = plane // LANES
    width = 2 * plane
    low = low_half(rows)
    some = min(ROWS, rows)
    steps = [(d, row) for row in range(0, vel, rows) for d in range(2)]
    slots = blocks.shape[0]

    def fetch(i):
        d, row = steps[i]
        at = part * vel + row
        return pltpu.make_async_copy(dist.at[d, at : at + rows, :], blocks.at[i % slots], arrived.at[i % slots])

    if part == 0:
        first = pltpu.make_async_copy(factors, table, read)
        first.start()
    for i in range(min(slots, len(steps))):
        fetch(i).start()
    if part == 0:
        first.wait()
        prepare(plane, parts, table, reach, gain, ends, spread)

    for i, (d, row) in enumerate(steps):
        fetch(i).wait()
        ref = blocks.at[i % slots]
        left = gain[d, part * vel + row : part * vel + row + rows, :]

        def gains(p):
            return dot(left, spread[:, p * width : (p + 1) * width])

        def load(p, t):
            return ref[:, p * width + t * LANES : p * width + (t + 1) * LANES]

        def store(p, t, value):
            swept[d, row : row + rows, p * width + t * LANES : p * width + (t + 1) * LANES] = value

        values = sweep_rows(rows, load, store, gains, d == 1, pairs, plane)
        if i + slots < len(steps):
            fetch(i + slots).start()
        full, half = packed_last(values, d == 1, whole, low)
        both = [
            jnp.where(low[: some // 2], half[n : n + some // 2], turn(half[n + some // 2 : n + some]))
            for n in range(0, rows, some)
        ]
        for s in range(1, count):
            out = sent[s - 1]

            @pl.when(((me ^ s) > me) == (d == 0))
            def _():
                for w in range(whole):
                    out[w * vel + row : w * vel + row + rows, :] = full[w]
                for n, packed in enumerate(both):
                    at = whole * vel + (row + n * some) // 2
                    out[at : at + some // 2, :] = packed

    tail = whole * vel + vel // 2
    for s in range(1, count):
        sent[s - 1][tail : tail + 8, :] = jnp.where((me ^ s) > me, ends[2 * part], ends[2 * part + 1])


def moment_kernel(plane, parts, reach, weight, *refs):
    sums = refs[:parts]
    out, high_lhs, rest_lhs, next_high, next_rest = refs[parts:]
    vel = sums[0].shape[1]
    k = weight.shape[1]
    width = 2 * plane
    pairs = next_high.shape[1] // k
    whole = plane // LANES
    low = low_half(k)
    for d in range(2):
        for p in range(pairs):
            rows = [weight[d] * reach[d, 2 * p : 2 * p + 1, :], weight[d] * reach[d, 2 * p + 1 : 2 * p + 2, :]]
            both = slice(2 * p * k, 2 * (p + 1) * k)
            high_lhs[d, both, :], rest_lhs[d, both, :] = halves(jnp.concatenate(rows, axis=0))
            q = p + 1 if d == 1 else p - 1
            if 0 <= q < pairs:
                at = slice(q * k, (q + 1) * k)
                next_high[d, at, :], next_rest[d, at, :] = halves(rows[d])
        q = 0 if d == 1 else pairs - 1
        at = slice(q * k, (q + 1) * k)
        next_high[d, at, :] = jnp.zeros((k, weight.shape[2]), bf16)
        next_rest[d, at, :] = jnp.zeros((k, weight.shape[2]), bf16)
    first = lax.broadcasted_iota(jnp.int32, (k, width), 1) < plane
    out[...] = jnp.zeros(out.shape, f32)

    def exchanged(x):
        tiles = [x[:, t : t + LANES] for t in range(0, width, LANES)]
        return jnp.concatenate(swap_cells(tiles, whole, low), axis=1)

    def pair(p):
        at = pl.ds(pl.multiple_of(p * width, width), width)
        ahead = jnp.minimum(p + 1, pairs - 1)
        behind = jnp.maximum(p - 1, 0)
        here = jnp.zeros((k, width), f32)
        for d in range(2):
            total = jnp.zeros((3 * k, width), f32)
            for c, part in enumerate(sums):
                high, rest = halves(part[d, :, at])
                cols = slice(c * vel, (c + 1) * vel)
                own = pl.ds(pl.multiple_of(p * 2 * k, 2 * k), 2 * k)
                after = pl.ds(pl.multiple_of(p * k, k), k)
                left = [high_lhs[d, own, cols], next_high[d, after, cols], rest_lhs[d, own, cols], next_rest[d, after, cols]]
                main = dot(jnp.concatenate(left, axis=0), high)
                total += main[: 3 * k] + main[3 * k :] + dot(jnp.concatenate(left[:2], axis=0), rest)
            even, odd, after = total[:k], total[k : 2 * k], total[2 * k :]
            if d == 0:
                here += jnp.where(first, even, odd + exchanged(odd))
                moved = jnp.where(first, exchanged(after), 0.0)
                out[:, pl.ds(pl.multiple_of(ahead * width, width), width)] += moved
            else:
                here += jnp.where(first, even + exchanged(even), odd)
                moved = jnp.where(first, 0.0, exchanged(after))
                out[:, pl.ds(pl.multiple_of(behind * width, width), width)] += moved
        out[:, at] += here

    @pl.loop(0, pairs // (2 * GROUP))
    def _(i):
        for u in range(2 * GROUP):
            pair(2 * GROUP * i + u)


def correct_kernel(plane, part, last, number, moments, high_lhs, rest_lhs, *refs):
    count = lax.axis_size("gx")
    refs_c, refs = refs[: count - 1], refs[count:]
    entering, outs, (natural, work) = refs[0], refs[1:-2], refs[-2:]
    me = lax.axis_index("gx")
    core = lax.axis_index("vert") % 2
    tiles, whole = 2 * plane // LANES, plane // LANES
    vel = entering.shape[1]
    k = moments.shape[0]
    pairs = moments.shape[1] // (2 * plane)
    rows = min(ROWS, vel)
    low = low_half(rows)
    tail = whole * vel + vel // 2
    passed = [r[tail : tail + 8, :] for r in refs_c]
    scale = []
    for s in range(1, count):
        q = me ^ s
        product = jnp.ones((8, LANES), f32)
        for z in range(1, count):
            if z != s:
                h = me ^ z
                between = ((q < h) & (h < me)) | ((me < h) & (h < q))
                product = product * jnp.where(between, passed[z - 1], 1.0)
        product = product * passed[s - 1]
        scale.append((jnp.where(q < me, product, 0.0), jnp.where(q > me, product, 0.0)))
    for sub in range(vel // rows):
        row = sub * rows
        full = [[jnp.zeros((rows, LANES), f32)] * whole for _ in range(2)]
        half = [jnp.zeros((rows, LANES), f32) for _ in range(2)]
        for s in range(1, count):
            ref = refs_c[s - 1]
            packed = ref[whole * vel + row // 2 : whole * vel + (row + rows) // 2, :]
            ends = jnp.concatenate([packed, turn(packed)], axis=0)
            for d in range(2):
                by = jnp.concatenate(
                    [
                        jnp.broadcast_to(scale[s - 1][d][:, j : j + 1], (8, LANES))
                        for j in range(row // 8, (row + rows) // 8)
                    ],
                    axis=0,
                )
                full[d] = [full[d][w] + by * ref[w * vel + row : w * vel + row + rows, :] for w in range(whole)]
                half[d] = half[d] + by * ends
        for d in range(2):
            cell = full[d] + [half[d]]
            for t in range(whole + 1):
                natural[d, row : row + rows, t * LANES : (t + 1) * LANES] = cell[t]
            turned = [turn(x) for x in cell]
            pair = full[d] + [jnp.where(low, half[d], turned[0])]
            for w in range(whole):
                pair.append(jnp.where(low, turned[w], turned[w + 1]))
            for t in range(tiles):
                entering[d, row : row + rows, t * LANES : (t + 1) * LANES] = pair[t]
    low = low_half(k)
    cols = slice(part * vel, (part + 1) * vel)
    for d in range(2):
        high, rest = halves(natural[d])
        total = dot(high_lhs[d, :, cols], high) + dot(rest_lhs[d, :, cols], high) + dot(high_lhs[d, :, cols], rest)
        if d == 0:
            work[...] = total
        else:
            work[...] += total
    half_pairs = pairs // 2
    width = 2 * plane

    def corrected(p):
        first, second = (
            [work[(2 * p + i) * k : (2 * p + i + 1) * k, t : t + LANES] for t in range(0, (whole + 1) * LANES, LANES)]
            for i in range(2)
        )
        turned = [turn(x) for x in second]
        term = first[:whole] + [jnp.where(low, first[whole], turned[0])]
        term += [jnp.where(low, turned[w], turned[w + 1]) for w in range(whole)]
        return moments[:, p * width : (p + 1) * width] + jnp.concatenate(term, axis=1)

    if not last:
        for p in range(pairs):
            outs[0][:, p * width : (p + 1) * width] = corrected(p)
        return
    half_tiles = half_pairs * width // LANES
    for n in range(2):

        @pl.when(core == n)
        def _():
            for p in range(pairs):
                out = outs[(p // half_pairs) ^ n]
                value = corrected(p)
                for t in range(width // LANES):
                    head, tail = packed_rows(p % half_pairs * (width // LANES) + t, half_tiles, number)
                    out[head, :] = value[:8, t * LANES : (t + 1) * LANES]
                    out[tail, :] = value[8:number, t * LANES : (t + 1) * LANES]


def fit_rows(m):
    density = 1.0 + 0.5 * jnp.tanh(m[0])
    u = [0.5 * jnp.tanh(m[j]) for j in (1, 2, 3)]
    inverse = 1.0 / (1.0 + 0.5 * jnp.tanh(m[4]))
    s = [0.2 * jnp.tanh(m[j]) for j in range(5, 10)]
    q = [0.2 * jnp.tanh(m[j]) for j in range(10, 13)]
    h = 0.5 * inverse
    uu = u[0] * u[0] + u[1] * u[1] + u[2] * u[2]
    qu = q[0] * u[0] + q[1] * u[1] + q[2] * u[2]
    e = h * 1.4426950408889634
    exponent = [-e * uu, 2.0 * e * u[0], 2.0 * e * u[1], 2.0 * e * u[2], -e, -e, -e]
    a = h * uu - 2.5
    xx, yy, zz = 0.5 * s[3], 0.5 * s[4], -0.5 * (s[3] + s[4])
    xy, xz, yz = s[0], s[1], s[2]
    gx = xx * u[0] + 0.5 * (xy * u[1] + xz * u[2])
    gy = yy * u[1] + 0.5 * (xy * u[0] + yz * u[2])
    gz = zz * u[2] + 0.5 * (xz * u[0] + yz * u[1])
    form = gx * u[0] + gy * u[1] + gz * u[2]
    two = 2.0 * h
    scale = density * inverse * jnp.sqrt(inverse)
    by = scale * inverse
    square = qu * h
    terms = [
        scale + by * (form - qu * a),
        by * (a * q[0] + two * qu * u[0] - 2.0 * gx),
        by * (a * q[1] + two * qu * u[1] - 2.0 * gy),
        by * (a * q[2] + two * qu * u[2] - 2.0 * gz),
        by * (xx - two * q[0] * u[0] - square),
        by * (yy - two * q[1] * u[1] - square),
        by * (zz - two * q[2] * u[2] - square),
        by * (xy - two * (q[0] * u[1] + q[1] * u[0])),
        by * (xz - two * (q[0] * u[2] + q[2] * u[0])),
        by * (yz - two * (q[1] * u[2] + q[2] * u[1])),
        by * (h * q[0]),
        by * (h * q[1]),
        by * (h * q[2]),
    ]
    return exponent, terms


def stacked_right(x):
    a, b, c = thirds(x)
    return jnp.concatenate([a, b, a, c, b, a, jnp.zeros((LANES - 96, x.shape[1]), bf16)], axis=0)


def table_kernel(velocity, relax, reach, _, left_e, left_p, left_r):
    for d in range(2):
        fraction = relax[d]
        x, y, z = (velocity[j, d] for j in range(3))
        xx, yy, zz = x * x, y * y, z * z
        square = xx + yy + zz
        rows = [jnp.ones_like(x), x, y, z, xx, yy, zz, x * y, x * z, y * z, x * square, y * square, z * square]
        rows = jnp.concatenate(rows + [jnp.zeros_like(x)] * (16 - len(rows)), axis=0)
        for ref, value in ((left_e, rows), (left_p, rows * fraction)):
            a, b, c = (t.astype(f32) for t in thirds(value))
            stack = [a, a, b, a, b, c]
            rest = ref.shape[2] - 16 * len(stack)
            if rest:
                stack.append(jnp.zeros((rest, value.shape[1]), f32))
            ref[d, :, :] = jnp.concatenate(stack, axis=0).T.astype(bf16)
        left_r[d, :, :] = turned_thirds(reach[d] * (1.0 - fraction), left_r.shape[2])


def fit_kernel(plane, k, own, rest, macro, right_e, right_p, tiles, turned, fitted):
    me, count = lax.axis_index("gx"), lax.axis_size("gx")
    core = lax.axis_index("vert") % 2
    lanes = macro.shape[1]
    margin = SMOOTH * plane // LANES
    inner = lanes // LANES
    half = inner // 2
    number = inner + 2 * margin
    whole = plane // LANES
    low = low_half(k)
    tile = lambda t: slice(t % number * k, t % number * k + k)
    column = lambda t: slice(t * LANES, (t + 1) * LANES)

    count_of = macro.shape[0]
    outside = eights(half * count_of)

    def place(t, ref, offset, of, size):
        at = t * k
        for piece, row in zip(packed_rows(of, size, count_of), (at, at + 8)):
            some = piece.stop - piece.start
            tiles[row : row + some, :] = ref[offset + piece.start : offset + piece.stop, :]

    for first, left, right in ((0, own, rest), (1, rest, own)):

        @pl.when(core == first)
        def _():
            for t in range(margin):
                place(t, left, outside, t, margin)
                place(margin + inner + t, right, outside, t, margin)
            for t in range(half):
                place(margin + t, left, 0, t, half)
                place(margin + half + t, right, 0, t, half)

    before = jnp.where(me > 0, RATE, 0.0)
    after = jnp.where(me < count - 1, RATE, 0.0)
    for _ in range(SMOOTH):
        for t in range(number):
            turned[tile(t), :] = turn(tiles[tile(t), :])
        for t in range(number):
            value = tiles[tile(t), :]
            behind = jnp.where(low, turned[tile(t - whole - 1), :], turned[tile(t - whole), :])
            ahead = jnp.where(low, turned[tile(t + whole), :], turned[tile(t + whole + 1), :])
            rate = (before if t < margin else after if t >= margin + inner else RATE) / (1.0 + value[0:1] * value[0:1])
            tiles[tile(t), :] = value + rate * (behind + ahead - 2.0 * value)

    fitted[...] = jnp.zeros(fitted.shape, f32)
    some = 8
    for t in range(0, inner, some):
        values = [tiles[pl.ds((margin + t) * k + j, some, stride=k), :] for j in range(macro.shape[0])]
        for n, group in enumerate(fit_rows(values)):
            for j, value in enumerate(group):
                fitted[pl.ds((n * inner + t) * k + j, some, stride=k), :] = value
    for t in range(inner):
        macro[:, column(t)] = tiles[tile(margin + t), :][: macro.shape[0]]
        for n, right in enumerate((right_e, right_p)):
            right[:, column(t)] = stacked_right(fitted[(n * inner + t) * k : (n * inner + t + 1) * k, :])


def join_kernel(plane, d, offset, span, sums, entering, left, spread, _, kept):
    vel = sums.shape[1]
    width = 2 * plane
    tiles, whole = width // LANES, plane // LANES
    pairs = sums.shape[2] // width
    rows = min(ROWS, vel)
    low = low_half(rows)

    def pair(i):
        p = i if d == 1 else pairs - 1 - i
        before = jnp.minimum(p + 1, pairs - 1) if d == 1 else jnp.maximum(p - 1, 0)
        there = jnp.where(i == pairs - 1, 0.0, 1.0)
        place = lambda q, t: pl.ds(pl.multiple_of(q * width + t * LANES, LANES), LANES)
        crossed = []
        for row in range(0, vel, rows):
            line = slice(row, row + rows)
            own = [sums[d, line, place(p, t)] for t in range(tiles)]
            past = [
                None if (t < whole) != (d == 1) and t != whole else there * sums[d, line, place(before, t)]
                for t in range(tiles)
            ]
            crossed.append(other_cell(own, past, d == 1, whole, low))
        right = spread[:, pl.ds(pl.multiple_of(p * width, width), width)]
        reach = dot(left[d, offset : offset + vel, :], right)
        for n, row in enumerate(range(0, vel, rows)):
            line = slice(row, row + rows)
            for t in range(tiles):
                tile = slice(t * LANES, (t + 1) * LANES)
                value = sums[d, line, place(p, t)] + crossed[n][t] + entering[d, line, tile]
                kept[d, line, place(p, t)] = reach[line, tile] * value

    @pl.loop(*span)
    def _(i):
        for u in range(GROUP):
            pair(i * GROUP + u)


def add_kernel(a, b, *refs):
    out = refs[-1]
    out[...] = a[...] + b[...]


def edge_kernel(margin, number, a, b, *refs):
    out, edge = refs[-2:]
    out[...] = a[...] + b[...]
    first = lax.axis_index("vert") % 2 == 0
    tiles = out.shape[0] // number
    rest = number - 8
    for start, size, into in ((0, 8, 0), (8 * tiles, rest, 8 * margin)):
        low = out[start : start + size * margin, :]
        high = out[start + size * (tiles - margin) : start + size * tiles, :]
        edge[into : into + size * margin, :] = jnp.where(first, low, high)
    if edge.shape[0] > number * margin:
        edge[number * margin :, :] = jnp.zeros((edge.shape[0] - number * margin, LANES), f32)


def close_kernel(a, b, halo, more, *refs):
    out, rows = refs[-1], a.shape[0]
    out[:rows, :] = a[...] + b[...]
    out[rows:, :] = halo[...] + more[...]


def finish_kernel(plane, parts, *refs):
    kept = refs[:parts]
    left_e, left_p, right_e, right_p, updated = refs[parts:]
    vel = kept[0].shape[1]
    width = 4 * plane
    block = min(vel, 2 * BLOCK)

    def body(*outs):
        at = pl.ds(pl.multiple_of(pl.program_id(0) * width, width), width)
        be, bp = right_e[:, at], right_p[:, at]
        for d in range(2):
            for c in range(parts):
                for row in range(0, vel, block):
                    there = slice(c * vel + row, c * vel + row + block)
                    equil = jnp.exp2(dot(left_e[d, there, :], be)) * dot(left_p[d, there, :], bp)
                    outs[d][there, :] = kept[c][d, row : row + block, at] + equil

    spec = lambda d: pl.BlockSpec((None, updated.shape[1], width), lambda i: (d, 0, i))
    pltpu.emit_pipeline(body, grid=(updated.shape[2] // width,), out_specs=[spec(0), spec(1)])(updated, updated)


def in_vmem(x):
    return pltpu.with_memory_space_constraint(x, pltpu.VMEM)


def per_device(dist, factors, velocity, weights, relax):
    _, vel, lanes = dist.shape
    cells = factors.shape[2]
    plane = lanes // cells
    count = lax.axis_size("gx")
    moments_n = weights.shape[0]
    k = 16
    pairs = cells // 2
    tiles, whole = 2 * plane // LANES, plane // LANES
    width = 2 * plane
    vel_part = vel // PARTS
    vmem = pl.BlockSpec(memory_space=pltpu.VMEM)
    anywhere = pl.BlockSpec(memory_space=pl.ANY)
    params = pltpu.CompilerParams(vmem_limit_bytes=12 * MIB)

    depth = -(-3 * cells // LANES) * LANES
    rows = min(BLOCK, vel_part)
    payload = whole * vel_part + vel_part // 2 + 8
    hbm = pl.BlockSpec(memory_space=pltpu.HBM)
    dist = pltpu.with_memory_space_constraint(dist, pltpu.HBM)
    table = pltpu.with_memory_space_constraint(jnp.swapaxes(factors, 1, 2), pltpu.HBM)
    shared = [
        jax.ShapeDtypeStruct((2, cells, vel), f32),
        pltpu.VMEM((2, vel, depth), bf16),
        pltpu.VMEM((2 * PARTS, 8, LANES), f32),
        pltpu.VMEM((depth, lanes), bf16),
    ]
    swept, sent = [], []
    for part in range(PARTS):
        out, *leaving = pl.pallas_call(
            lambda *refs, part=part: sweep_kernel(part, rows, plane, PARTS, count, *refs),
            out_shape=[pltpu.VMEM((2, vel_part, lanes), f32)]
            + [jax.ShapeDtypeStruct((payload, LANES), f32)] * (count - 1)
            + ([] if part else shared),
            in_specs=[hbm] + ([vmem] * 3 if part else [hbm]),
            out_specs=[vmem] * (count + (0 if part else len(shared))),
            scratch_shapes=[pltpu.VMEM((3, rows, lanes), f32), pltpu.SemaphoreType.DMA((3,))]
            + ([] if part else [pltpu.VMEM((2, cells, vel), f32), pltpu.SemaphoreType.DMA(())]),
            compiler_params=params,
            name="sweep",
        )(dist, *([gain, ends, spread] if part else [table]))
        if part == 0:
            leaving, (reach, gain, ends, spread) = leaving[: count - 1], leaving[count - 1 :]
            gain, ends, spread = in_vmem(gain), in_vmem(ends), in_vmem(spread)
        swept.append(in_vmem(out))
        sent.append(leaving)

    padded = jnp.pad(jnp.moveaxis(weights, 1, 0), ((0, 0), (0, k - moments_n), (0, 0)))
    moments, *lhs = pl.pallas_call(
        lambda *refs: moment_kernel(plane, PARTS, *refs),
        out_shape=[jax.ShapeDtypeStruct((k, lanes), f32)]
        + [pltpu.VMEM((2, 2 * pairs * k, vel), bf16)] * 2,
        in_specs=[vmem] * (2 + PARTS),
        out_specs=[vmem] * 3,
        scratch_shapes=[pltpu.VMEM((2, pairs * k, vel), bf16)] * 2,
        compiler_params=params,
        name="moments",
    )(reach, padded, *swept)

    left_e, left_p, left_r = pl.pallas_call(
        table_kernel,
        out_shape=[pltpu.VMEM((2, vel, LANES), bf16)] * 2 + [pltpu.VMEM((2, vel, depth), bf16)],
        in_specs=[vmem] * 3 + [anywhere],
        out_specs=[vmem] * 3,
        compiler_params=params,
        name="tables",
    )(velocity[:, :, None, :], relax[:, None, :], reach, moments)

    margin = SMOOTH * plane // LANES
    half = (eights(lanes // 2 // LANES * moments_n), LANES)
    side = (eights(margin * moments_n), LANES)
    kept = list(swept)

    def join(part, d, start, stop, after):
        span = tuple(x * (pairs // GROUP) // 4 for x in (start, stop))
        kept[part] = pl.pallas_call(
            lambda *refs: join_kernel(plane, d, part * vel_part, span, *refs),
            out_shape=pltpu.VMEM(kept[part].shape, f32),
            in_specs=[vmem] * 4 + [anywhere],
            out_specs=vmem,
            input_output_aliases={0: 0},
            compiler_params=params,
            cost_estimate=pl.CostEstimate(
                flops=dist.size * LANES * (stop - start) // (2 * PARTS),
                bytes_accessed=dist.size * (stop - start) // PARTS,
                transcendentals=0,
            ),
            name="join",
        )(in_vmem(kept[part]), entering[part], in_vmem(left_r), spread, after)
        return in_vmem(kept[part])

    entering = []
    for part in range(PARTS):
        last = part == PARTS - 1
        got = [
            lax.ppermute(sent[part][s - 1], "gx", [(i, i ^ s) for i in range(count)]) for s in range(1, count)
        ]
        out = [jax.ShapeDtypeStruct(half, f32)] * 2 if last else [jax.ShapeDtypeStruct((k, lanes), f32)]
        found, *moments = pl.pallas_call(
            lambda *refs, part=part, last=last: correct_kernel(plane, part, last, moments_n, *refs),
            out_shape=[pltpu.VMEM((2, vel_part, width), f32)] + out,
            in_specs=[vmem] * (3 + len(got)) + [anywhere],
            out_specs=[vmem] * (1 + len(out)),
            scratch_shapes=[
                pltpu.VMEM((2, vel_part, (whole + 1) * LANES), f32),
                pltpu.VMEM((2 * pairs * k, (whole + 1) * LANES), f32),
            ],
            compiler_params=params,
            name="correct",
        )(*(moments if part else [moments]), *[in_vmem(x) for x in lhs], *got, early if part else left_r)
        entering.append(in_vmem(found))
        if not last:
            early = join(part, 0, 0, 2, found)
    mine, other = moments

    size = lax.axis_size("vert")
    def combine(kernel, out, *args):
        done = [x for x in args if x is not None]
        return pl.pallas_call(
            kernel,
            out_shape=[jax.ShapeDtypeStruct(x, f32) for x in out],
            in_specs=[vmem] * len(done),
            out_specs=[vmem] * len(out),
            compiler_params=params,
            name="add",
        )(*done)

    steps = [1]
    while 2 * steps[-1] < size:
        steps.append(2 * steps[-1])
    total, beside = mine, None
    for i, step in enumerate(steps[:-1]):
        got = lax.ppermute(total if i else other, "vert", [(v, v ^ step) for v in range(size)])
        if i == 1:
            join(0, 0, 2, 4, total)
            beside = join(0, 1, 0, 2, total)
        if i == len(steps) - 2:
            total, edge = combine(
                lambda *refs: edge_kernel(margin, moments_n, *refs), [half, side], total, got, beside
            )
        else:
            (total,) = combine(add_kernel, [half], total, got, beside)
    step = steps[-1]
    got = lax.ppermute(total, "vert", [(v, v ^ step) for v in range(size)])
    beyond = []
    for g in range(count - 1):
        for v in range(1, size, 2):
            near, far = g * size + v, (g + 1) * size + v - 1
            beyond += [(near, far), (far, near)]
    halo = lax.ppermute(edge, ("gx", "vert"), beyond)
    join(1, 0, 0, 4, total)
    more = lax.ppermute(halo, "vert", [(v, v ^ step) for v in range(size)])
    join(0, 1, 2, 4, halo)
    join(1, 1, 0, 2, halo)
    (own,) = combine(close_kernel, [(half[0] + side[0], LANES)], total, got, halo, more, *[in_vmem(x) for x in kept])
    rest = lax.ppermute(own, "vert", [(v, v ^ 1) for v in range(size)])
    join(1, 1, 2, 4, own)

    macro, right_e, right_p = pl.pallas_call(
        lambda *refs: fit_kernel(plane, k, *refs),
        out_shape=[jax.ShapeDtypeStruct((moments_n, lanes), f32)] + [pltpu.VMEM((LANES, lanes), bf16)] * 2,
        in_specs=[vmem] * 2,
        out_specs=[vmem] * 3,
        scratch_shapes=[pltpu.VMEM((((lanes // LANES) + 2 * margin) * k, LANES), f32)] * 2
        + [pltpu.VMEM((2 * lanes // LANES * k, LANES), f32)],
        compiler_params=params,
        name="fit",
    )(own, rest)

    last = [*kept, left_e, left_p, right_e, right_p]
    updated = pl.pallas_call(
        lambda *refs: finish_kernel(plane, PARTS, *refs),
        out_shape=jax.ShapeDtypeStruct(dist.shape, f32),
        in_specs=[vmem] * len(last),
        out_specs=anywhere,
        compiler_params=params,
        name="finish",
    )(*[in_vmem(x) for x in last])
    return updated, macro


def solution(mesh):
    return jax.shard_map(
        per_device,
        mesh=mesh,
        in_specs=(
            P(None, "vert", "gx"),
            P(None, "vert", "gx"),
            P(None, None, "vert"),
            P(None, None, "vert"),
            P(None, "vert"),
        ),
        out_specs=(P(None, "vert", "gx"), P(None, "gx")),
        check_vma=False,
    )
```
